512 devices in a mesh: row: 32 (over x, z_hi, core), col: 16 (over y, z_lo).
Axes of the slice: x: 4, y: 8, z: 8 (z_hi: 4, z_lo: 2; z = z_hi * 2 + z_lo), core: 2. Of those that a mesh axis runs over, the one named last changes fastest.
Arguments:
- layer_input: bfloat16 [1024, 6144], P('row', 'col'), may hold values from -6 to 6
- output_grad: bfloat16 [1024, 6144], P('row', 'col'), may hold values from -1.5 to 1.5
- preact: bfloat16 [1024, 24576], P('col', 'row'), may hold values from -8 to 8
- weight_in: bfloat16 [6144, 24576], P('col', 'row'), may hold values from -0.078125 to 0.078125
- weight_out: bfloat16 [24576, 6144], P('row', 'col'), may hold values from -0.0390625 to 0.0390625
Outputs:
- input_grad: bfloat16 [1024, 6144], P('row', 'col')
- grad_in: float32 [6144, 24576], P('col', 'row')
- grad_out: float32 [24576, 6144], P('row', 'col')
The draws below stay inside these ranges and needn't reach their ends.
All inputs are finite; a program needn't handle non-finite values.
Results may differ from the reference program's by a relative error of at most 0.0049.
Values may be sent and summed in bfloat16 or wider, within the bound.
A program may use at most 64 MiB of HBM per device.

```python
import math
import jax
import jax.numpy as jnp

D = 6144
FF = 24576
TOKENS = 1024


def level_of(rng, shape, pieces, least, largest):
    level, own = 1.0, jax.random.fold_in(rng, 6)
    for axis_at, shards_of in pieces:
        heights = jnp.exp(jax.random.uniform(jax.random.fold_in(own, axis_at), (shards_of,), jnp.float32, least / len(pieces), largest / len(pieces)))
        level = level * jnp.repeat(heights, shape[axis_at] // shards_of).reshape([-1 if axis == axis_at else 1 for axis in range(len(shape))])
    return level


def bell_draw(rng, shape, spread, most, shards=(), dtype=jnp.bfloat16):
    drawn = jax.random.normal(rng, shape, jnp.float32) * spread
    if len(shards) > 0:
        drawn = level_of(rng, shape, shards, -0.22, 0.18) * drawn
    return jnp.clip(drawn, min=-most, max=most).astype(dtype)


def setup_inputs(seed: int = 0) -> dict:
    streams_of = jax.random.split(jax.random.key(seed), 6)
    layer_input = bell_draw(streams_of[0], (TOKENS, D), 1.0, 6.0, ((0, 32), (1, 16)))
    output_grad = bell_draw(streams_of[1], (TOKENS, D), 0.25, 1.5, ((0, 32), (1, 16)))
    preact = bell_draw(streams_of[2], (TOKENS, FF), 1.5, 8.0, ((0, 16), (1, 32)))
    weight_in = bell_draw(streams_of[3], (D, FF), D ** -0.5, 0.078125, ((0, 16), (1, 32)))
    weight_out = bell_draw(streams_of[4], (FF, D), FF ** -0.5, 0.0390625, ((0, 32), (1, 16)))
    return {"layer_input": layer_input, "output_grad": output_grad, "preact": preact, "weight_in": weight_in, "weight_out": weight_out}


def gelu_parts(pre):
    cdf = 0.5 * (1.0 + jax.scipy.special.erf(pre / math.sqrt(2.0)))
    pdf = jnp.exp(-0.5 * pre * pre) / math.sqrt(2.0 * math.pi)
    return (pre * cdf, cdf + pre * pdf)

def reference(layer_input, output_grad, preact, weight_in, weight_out):
    pre = preact.astype(jnp.float32)
    value, slope = gelu_parts(pre)
    activ = value.astype(jnp.bfloat16)
    act_grad = jnp.dot(output_grad, weight_out.T, preferred_element_type=jnp.float32)
    hid_grad = (act_grad * slope).astype(jnp.bfloat16)
    grad_out = jnp.dot(activ.T, output_grad, preferred_element_type=jnp.float32)
    grad_in = jnp.dot(layer_input.T, hid_grad, preferred_element_type=jnp.float32)
    input_grad = jnp.dot(hid_grad, weight_in.T, preferred_element_type=jnp.float32).astype(jnp.bfloat16)
    return (input_grad, grad_in, grad_out)
```

```python
import math

import jax
import jax.numpy as jnp
from jax import lax
from jax.experimental import pallas as pl
from jax.experimental.pallas import tpu as pltpu
from jax.sharding import PartitionSpec as P

MESH = pl.DeviceIdType.MESH
BF, F32 = jnp.bfloat16, jnp.float32
TOK, DB, FB = 1024, 384, 768
T = 32
DELTAS = [(dx, dz) for dx in (2, 1, 3, 0) for dz in (2, 1, 3, 0) if (dx, dz) != (0, 0)]


def gelu_parts(pre):
    cdf = 0.5 * (1.0 + lax.erf(pre * (1.0 / math.sqrt(2.0))))
    pdf = jnp.exp(-0.5 * pre * pre) * (1.0 / math.sqrt(2.0 * math.pi))
    return pre * cdf, cdf + pre * pdf


def dot(a, b, ca, cb):
    return lax.dot_general(a, b, (((ca,), (cb,)), ((), ())), preferred_element_type=F32)


def kernel(
    li, og, pre, w_in_hbm, w_out_hbm, ig_out, gi_out, go_out,
    w_in, w_out, li_all, og_all, act_all, hid_all, li_t, slope, c_own, cz_send, cz_recv, r_send, r_recv,
    q_sib, q_in, q_own, q_send, q_recv, gi_v, go_v,
    og_ss, og_rs, ogs_ss, ogs_rs, li_ss, li_rs, lis_ss, lis_rs, ar_ss, ar_rs, az_ss, az_rs, hr_ss, hr_rs, hz_ss, hz_rs,
    cz_ss, cz_rs, rr_ss, rr_rs, qs_ss, qs_rs, q_ss, q_rs, loc,
):
    row, col = lax.axis_index("row"), lax.axis_index("col")
    x, zh, k = row // 8, (row // 2) % 4, row % 2
    y, zl = col // 2, col % 2

    def dev(x=x, zh=zh, k=k, y=y, zl=zl):
        return (x * 8 + zh * 2 + k, y * 2 + zl)

    sib, zpart = dev(k=1 - k), dev(zl=1 - zl)
    ynext = [dev(y=(y + 1) % 8), dev(y=(y + 7) % 8)]

    def peer(dx, dz):
        return (x + dx) % 4, (zh + dz) % 4

    def place(px, pz):
        return pz % 2, px * 2 + pz // 2

    mine = place(x, zh)
    started = []

    def send(src, dst, ss, rs, to):
        c = pltpu.make_async_remote_copy(src_ref=src, dst_ref=dst, send_sem=ss, recv_sem=rs, device_id=to, device_id_type=MESH)
        c.start()
        started.append(c)

    def arrive(dst, ss, rs):
        pltpu.make_async_remote_copy(src_ref=dst, dst_ref=dst, send_sem=ss, recv_sem=rs, device_id=sib, device_id_type=MESH).wait_recv()

    load_out = pltpu.make_async_copy(w_out_hbm, w_out, loc.at[0])
    load_in = pltpu.make_async_copy(w_in_hbm, w_in, loc.at[1])
    load_out.start()
    load_in.start()

    barrier = pltpu.get_barrier_semaphore()
    partners = [dev(x=px, zh=pz) for px, pz in (peer(*d) for d in DELTAS)] + [sib, zpart] + ynext
    for p in partners:
        pl.semaphore_signal(barrier, inc=1, device_id=p, device_id_type=MESH)

    og_all[k, mine[0], mine[1]] = og[...]
    li_all[k, mine[0], mine[1]] = li[...]
    for h in range(2):
        value, sl = gelu_parts(pre[pl.ds(h * T, T), :].astype(F32))
        act_all[h, zl, y] = value.astype(BF)
        slope[h] = sl
    pl.semaphore_wait(barrier, len(partners))

    def gather_send(own, full, ss, rs):
        for j, d in enumerate(DELTAS):
            px, pz = peer(*d)
            send(own, full.at[k, mine[0], mine[1]], ss.at[j], rs.at[j], dev(x=px, zh=pz))

    def gather_arrive(full, ss, rs, sss, srs):
        for j, d in enumerate(DELTAS):
            p = place(*peer(-d[0] + 4, -d[1] + 4))
            arrive(full.at[k, p[0], p[1]], ss.at[j], rs.at[j])
        send(full.at[k], full.at[k], sss, srs, sib)

    def gather_done(full, sss, srs):
        arrive(full.at[1 - k], sss, srs)

    def ring_step(full, s, rss, rrs, z=None):
        for h in range(2):
            for d in range(2):
                sg = 1 - 2 * d
                came = (y - sg * s + 8) % 8
                if s == 0:
                    ref = full.at[h, zl, y]
                elif s <= 3 or h == d:
                    ref = full.at[h, zl, came]
                    arrive(ref, rss.at[d, s - 1, h], rrs.at[d, s - 1, h])
                else:
                    continue
                if s <= 2 or (s == 3 and h == d):
                    send(ref, ref, rss.at[d, s, h], rrs.at[d, s, h], ynext[d])
                if z is not None:
                    pass_on(full, s, d, h, *z)

    def slot(s, d):
        return 0 if s == 0 else 7 if s == 4 else s + 3 * d

    def pass_on(full, s, d, h, zss, zrs):
        if (s == 0 and d == 1) or (s == 4 and h != d):
            return
        ref = full.at[h, zl, (y - (1 - 2 * d) * s + 8) % 8]
        send(ref, ref, zss.at[slot(s, d), h], zrs.at[slot(s, d), h], zpart)

    def passed(full, zss, zrs):
        for s in range(5):
            for d in range(2):
                for h in range(2):
                    if (s == 0 and d == 1) or (s == 4 and h != d):
                        continue
                    ref = full.at[h, 1 - zl, (y - (1 - 2 * d) * s + 8) % 8]
                    arrive(ref, zss.at[slot(s, d), h], zrs.at[slot(s, d), h])

    act_z, hid_z = (az_ss, az_rs), (hz_ss, hz_rs)
    gather_send(og, og_all, og_ss, og_rs)
    ring_step(act_all, 0, ar_ss, ar_rs, act_z)
    gather_arrive(og_all, og_ss, og_rs, ogs_ss, ogs_rs)
    ring_step(act_all, 1, ar_ss, ar_rs, act_z)

    load_out.wait()

    def partial(h, half, store):
        rows = og_all[h, half].reshape(8 * T, DB)

        def tile(n, _):
            cols = pl.ds(pl.multiple_of(n * 256, 256), 256)
            store(cols, dot(rows, w_out[cols, :], 1, 1).reshape(8, T, 256))
            return _

        lax.fori_loop(0, 3, tile, 0)

    def to_partner(h):
        def store(cols, v):
            cz_send[h, :, :, cols] = v.astype(BF)

        partial(h, 1 - zl, store)
        for d in (4, 3, 5, 2, 6, 1, 7, 0):
            at = (y + d) % 8
            send(cz_send.at[h, at], cz_recv.at[h, at], cz_ss.at[d, h], cz_rs.at[d, h], zpart)

    def to_self(h):
        def store(cols, v):
            c_own[h, :, :, cols] = v

        partial(h, zl, store)

    to_partner(k)
    gather_done(og_all, ogs_ss, ogs_rs)
    to_partner(1 - k)
    to_self(k)
    to_self(1 - k)
    ring_step(act_all, 2, ar_ss, ar_rs)

    def term(d, h):
        at = (y + d) % 8
        arrive(cz_recv.at[h, at], cz_ss.at[d, h], cz_rs.at[d, h])
        return c_own[h, at] + cz_recv[h, at].astype(F32)

    for s in range(4):
        for d in range(2):
            sg = 1 - 2 * d
            for h in (d, 1 - d):
                if s == 0 and h != d:
                    continue
                total = term((sg * (4 - s)) % 8, h)
                if s >= 2 or (s == 1 and h == d):
                    arrive(r_recv.at[d, s - 1, h], rr_ss.at[d, s - 1, h], rr_rs.at[d, s - 1, h])
                    total = total + r_recv[d, s - 1, h].astype(F32)
                r_send[d, s, h] = total.astype(BF)
                send(r_send.at[d, s, h], r_recv.at[d, s, h], rr_ss.at[d, s, h], rr_rs.at[d, s, h], ynext[d])
        if s == 0:
            gather_send(li, li_all, li_ss, li_rs)
        if s == 1:
            ring_step(act_all, 3, ar_ss, ar_rs)
        if s == 2:
            ring_step(act_all, 4, ar_ss, ar_rs)
            for t in (2, 3, 4):
                for d in range(2):
                    for h in range(2):
                        pass_on(act_all, t, d, h, *act_z)
    for h in range(2):
        total = term(0, h)
        for d in range(2):
            arrive(r_recv.at[d, 3, h], rr_ss.at[d, 3, h], rr_rs.at[d, 3, h])
            total = total + r_recv[d, 3, h].astype(F32)
        hid_all[h, zl, y] = (total * slope[h]).astype(BF)

    ring_step(hid_all, 0, hr_ss, hr_rs, hid_z)
    gather_arrive(li_all, li_ss, li_rs, lis_ss, lis_rs)
    passed(act_all, az_ss, az_rs)
    ring_step(hid_all, 1, hr_ss, hr_rs, hid_z)

    def go_tile(n, _):
        cols = pl.ds(pl.multiple_of(n * 256, 256), 256)
        go_v[cols, :] = dot(act_all[:, :, :, :, cols].reshape(TOK, 256), og_all[...].reshape(TOK, DB), 0, 0)
        return _

    lax.fori_loop(0, 3, go_tile, 0)
    store_go = pltpu.make_async_copy(go_v, go_out, loc.at[2])
    store_go.start()
    ring_step(hid_all, 2, hr_ss, hr_rs, hid_z)
    gather_done(li_all, lis_ss, lis_rs)
    li_t[...] = li_all[...].reshape(TOK, DB).T
    load_in.wait()
    ring_step(hid_all, 3, hr_ss, hr_rs, hid_z)
    ring_step(hid_all, 4, hr_ss, hr_rs, hid_z)

    def q_part(h, half):
        return dot(hid_all[h, half].reshape(8 * T, FB), w_in[...], 1, 1).reshape(8, T, DB)

    q_sib[zl] = q_part(1 - k, zl)
    send(q_sib.at[zl], q_in.at[zl], qs_ss.at[0], qs_rs.at[0], sib)
    q_own[zl] = q_part(k, zl)
    passed(hid_all, hz_ss, hz_rs)
    q_sib[1 - zl] = q_part(1 - k, 1 - zl)
    send(q_sib.at[1 - zl], q_in.at[1 - zl], qs_ss.at[1], qs_rs.at[1], sib)
    q_own[1 - zl] = q_part(k, 1 - zl)
    arrive(q_in.at[zl], qs_ss.at[0], qs_rs.at[0])
    arrive(q_in.at[1 - zl], qs_ss.at[1], qs_rs.at[1])
    q_send[...] = (q_own[...] + q_in[...]).astype(BF)
    for j, d in enumerate(DELTAS):
        px, pz = peer(*d)
        p = place(px, pz)
        send(q_send.at[p[0], p[1]], q_recv.at[j], q_ss.at[j], q_rs.at[j], dev(x=px, zh=pz))

    def gi_tile(n, _):
        cols = pl.ds(pl.multiple_of(n * 256, 256), 256)
        gi_v[:, cols] = dot(li_t[...], hid_all[:, :, :, :, cols].reshape(TOK, 256), 1, 0)
        return _

    lax.fori_loop(0, 3, gi_tile, 0)
    store_gi = pltpu.make_async_copy(gi_v, gi_out, loc.at[3])
    store_gi.start()

    total = q_own[mine[0], mine[1]] + q_in[mine[0], mine[1]]
    for j in range(len(DELTAS)):
        arrive(q_recv.at[j], q_ss.at[j], q_rs.at[j])
        total = total + q_recv[j].astype(F32)
    ig_out[...] = total.astype(BF)
    for c in started:
        c.wait_send()
    store_go.wait()
    store_gi.wait()


def on_device(layer_input, output_grad, preact, weight_in, weight_out):
    vmem, hbm = pl.BlockSpec(memory_space=pltpu.VMEM), pl.BlockSpec(memory_space=pl.ANY)
    dma = pltpu.SemaphoreType.DMA
    n = len(DELTAS)
    return pl.pallas_call(
        kernel,
        out_shape=(
            jax.ShapeDtypeStruct((T, DB), BF),
            jax.ShapeDtypeStruct((DB, FB), F32),
            jax.ShapeDtypeStruct((FB, DB), F32),
        ),
        in_specs=[vmem, vmem, vmem, hbm, hbm],
        out_specs=(vmem, hbm, hbm),
        scratch_shapes=[
            pltpu.VMEM((DB, FB), BF),
            pltpu.VMEM((FB, DB), BF),
            pltpu.VMEM((2, 2, 8, T, DB), BF),
            pltpu.VMEM((2, 2, 8, T, DB), BF),
            pltpu.VMEM((2, 2, 8, T, FB), BF),
            pltpu.VMEM((2, 2, 8, T, FB), BF),
            pltpu.VMEM((DB, TOK), BF),
            pltpu.VMEM((2, T, FB), F32),
            pltpu.VMEM((2, 8, T, FB), F32),
            pltpu.VMEM((2, 8, T, FB), BF),
            pltpu.VMEM((2, 8, T, FB), BF),
            pltpu.VMEM((2, 4, 2, T, FB), BF),
            pltpu.VMEM((2, 4, 2, T, FB), BF),
            pltpu.VMEM((2, 8, T, DB), F32),
            pltpu.VMEM((2, 8, T, DB), F32),
            pltpu.VMEM((2, 8, T, DB), F32),
            pltpu.VMEM((2, 8, T, DB), BF),
            pltpu.VMEM((n, T, DB), BF),
            pltpu.VMEM((DB, FB), F32),
            pltpu.VMEM((FB, DB), F32),
            dma((n,)), dma((n,)), dma, dma, dma((n,)), dma((n,)), dma, dma,
            dma((2, 4, 2)), dma((2, 4, 2)), dma((8, 2)), dma((8, 2)),
            dma((2, 4, 2)), dma((2, 4, 2)), dma((8, 2)), dma((8, 2)),
            dma((8, 2)), dma((8, 2)), dma((2, 4, 2)), dma((2, 4, 2)),
            dma((2,)), dma((2,)), dma((n,)), dma((n,)), dma((4,)),
        ],
        compiler_params=pltpu.CompilerParams(collective_id=0, has_side_effects=True, vmem_limit_bytes=48 * 2**20),
        cost_estimate=pl.CostEstimate(flops=8 * TOK * DB * FB, bytes_accessed=4 * 2**20, transcendentals=2 * 64 * FB),
        name="mlp_backward",
    )(layer_input, output_grad, preact, weight_in, weight_out)


def solution(mesh):
    in_specs = (P("row", "col"), P("row", "col"), P("col", "row"), P("col", "row"), P("row", "col"))
    out_specs = (P("row", "col"), P("col", "row"), P("row", "col"))
    return jax.shard_map(on_device, mesh=mesh, in_specs=in_specs, out_specs=out_specs, check_vma=False)
```

```python
import math

import jax
import jax.numpy as jnp
from jax import lax
from jax.experimental import pallas as pl
from jax.experimental.pallas import tpu as pltpu
from jax.sharding import PartitionSpec as P

MESH = pl.DeviceIdType.MESH
BF, F32 = jnp.bfloat16, jnp.float32
TOK, DB, FB = 1024, 384, 768
T = 32
FT = 256


def gelu_parts(pre):
    cdf = 0.5 * (1.0 + lax.erf(pre * (1.0 / math.sqrt(2.0))))
    pdf = jnp.exp(-0.5 * pre * pre) * (1.0 / math.sqrt(2.0 * math.pi))
    return pre * cdf, cdf + pre * pdf


def dot(a, b, ca, cb):
    return lax.dot_general(a, b, (((ca,), (cb,)), ((), ())), preferred_element_type=F32)


def kernel(
    li, og, pre, w_in_hbm, w_out_hbm, ig_out, gi_out, go_out,
    li_v, og_v, pre_v, ig_v, w_in, w_out, og2, li_all, og_all, act_all, hid_all, li_t, slope, c_own, r_send, r_recv,
    q_sib, q_in, q_send, q_recv, q_self, gi_v, go_v,
    gz_ss, gz_rs, gx_ss, gx_rs, gs_ss, gs_rs, oz_ss, oz_rs, ox_ss, ox_rs, os_ss, os_rs, lz_ss, lz_rs, lx_ss, lx_rs, ls_ss, ls_rs,
    az_ss, az_rs, ay_ss, ay_rs, hy_ss, hy_rs, hz_ss, hz_rs, wo_ss, wo_rs, wi_ss, wi_rs, rr_ss, rr_rs,
    qs_ss, qs_rs, q_ss, q_rs, loc,
):
    row, col = lax.axis_index("row"), lax.axis_index("col")
    x, zh, k = row // 8, (row // 2) % 4, row % 2
    y, zl = col // 2, col % 2
    halves = (1 - k, k)
    my = 2 * x + zh // 2
    same = zh % 2 == zl
    odd = (zh + zl) % 2

    def dev(x=x, zh=zh, k=k, y=y, zl=zl):
        return (x * 8 + zh * 2 + k, y * 2 + zl)

    sib, zpart = dev(k=1 - k), dev(zl=1 - zl)
    ynext = [dev(y=(y + 1) % 8), dev(y=(y + 7) % 8)]
    started = []

    def send(src, dst, ss, rs, to, cond=None):
        c = pltpu.make_async_remote_copy(src_ref=src, dst_ref=dst, send_sem=ss, recv_sem=rs, device_id=to, device_id_type=MESH)
        if cond is None:
            c.start()
        else:
            pl.when(cond)(c.start)
        started.append((cond, c))

    def arrive(dst, ss, rs):
        pltpu.make_async_remote_copy(src_ref=dst, dst_ref=dst, send_sem=ss, recv_sem=rs, device_id=sib, device_id_type=MESH).wait_recv()

    loads = [
        pltpu.make_async_copy(a, b, loc.at[i])
        for i, (a, b) in enumerate([(og, og_v), (pre, pre_v), (w_out_hbm, w_out.at[zl]), (w_in_hbm, w_in.at[zl]), (li, li_v)])
    ]
    for c in loads:
        c.start()

    barrier = pltpu.get_barrier_semaphore()
    greet = [dev(zh=(zh + a) % 4, zl=(zl + b) % 2) for a in range(4) for b in range(2) if (a, b) != (0, 0)]
    greet += [dev(x=(x + a) % 4, k=c) for a in (1, 2, 3) for c in (k, 1 - k)] + ynext + [sib]
    greet += [dev(x=(x + a) % 4, zh=b, zl=zh % 2) for a in (1, 2, 3) for b in range(4)]
    for p in greet:
        pl.semaphore_signal(barrier, inc=1, device_id=p, device_id_type=MESH)
    loads[0].wait()
    pl.semaphore_wait(barrier, len(greet))

    for dz in (2, 1, 3):
        send(og_v, og2.at[zl, k, my], gz_ss.at[dz], gz_rs.at[zl, dz], dev(zh=(zh + dz) % 4, zl=zh % 2))
    send(og_v, og2.at[zl, k, my], gz_ss.at[0], gz_rs.at[zl, 0], dev(zl=zh % 2), jnp.logical_not(same))

    @pl.when(same)
    def _():
        og2[zl, k, my] = og_v[...]

    for n in range(3):
        rows = pl.ds(n * FT, FT)
        send(w_out_hbm.at[rows], w_out.at[zl, rows], wo_ss.at[n], wo_rs.at[n], zpart)

    loads[1].wait()
    for h in range(2):
        value, sl = gelu_parts(pre_v[pl.ds(h * T, T), :].astype(F32))
        act_all[zl, h, y] = value.astype(BF)
        slope[h] = sl

    def act_step(j, s):
        zz = zl if j == 0 else 1 - zl
        for h in range(2):
            if s == 0 and j == 0:
                ref = act_all.at[zl, h, y]
                send(ref, ref, az_ss.at[h], az_rs.at[h], zpart)
            if s == 0 and j == 1:
                arrive(act_all.at[zz, h, y], az_ss.at[h], az_rs.at[h])
            for d in range(2):
                hops = 4 if h == d else 3
                ref = act_all.at[zz, h, (y + (8 - s if d == 0 else s)) % 8]
                if 0 < s <= hops:
                    arrive(ref, ay_ss.at[j, d, s - 1, h], ay_rs.at[j, d, s - 1, h])
                if s < hops:
                    send(ref, ref, ay_ss.at[j, d, s, h], ay_rs.at[j, d, s, h], ynext[d])

    act_step(0, 0)

    def source(e):
        dz = 2 * e + odd
        return dz, (zh + 4 - dz) % 4 // 2

    for e in range(2):
        for zs in range(2):
            dz, p = source(e)
            ref = og2.at[zs, k, 2 * x + p]
            if e == 0:

                @pl.when(jnp.logical_not(same & (zl == zs)))
                def _():
                    arrive(ref, gz_ss.at[0], gz_rs.at[zs, dz])

            else:
                arrive(ref, gz_ss.at[0], gz_rs.at[zs, dz])
            for dx in (2, 1, 3, 0):
                send(ref, ref, gx_ss.at[dx, e, zs], gx_rs.at[dx, e, zs], dev(x=(x + dx) % 4, k=1 - k))
    act_step(1, 0)
    act_step(0, 1)

    for dx in (0, 1, 3, 2):
        xs = (x + 4 - dx) % 4
        for zs in range(2):
            for e in range(2):
                arrive(og2.at[zs, 1 - k, 2 * xs + source(e)[1]], gx_ss.at[dx, e, zs], gx_rs.at[dx, e, zs])
            if dx > 0:
                ref = og2.at[zs, 1 - k, pl.ds(2 * xs, 2)]
                send(ref, ref, gs_ss.at[dx - 1, zs], gs_rs.at[dx - 1, zs], sib)
    act_step(1, 1)
    act_step(0, 2)

    loads[2].wait()

    def partial(a):
        h = halves[a]
        for n in range(3):
            rows = pl.ds(n * FT, FT)
            if a == 0:
                arrive(w_out.at[1 - zl, rows], wo_ss.at[n], wo_rs.at[n])
            total = dot(og2[0, h].reshape(8 * T, DB), w_out[0, rows, :], 1, 1)
            total += dot(og2[1, h].reshape(8 * T, DB), w_out[1, rows, :], 1, 1)
            c_own[h, :, :, rows] = total.reshape(8, T, FT)

    def rs_step(a, s):
        h = halves[a]
        for d in range(2):
            hops = 4 if a == d else 3
            if s >= hops:
                continue
            to = hops - s
            total = c_own[h, (y + (to if d == 0 else 8 - to)) % 8]
            if s > 0:
                arrive(r_recv.at[d, s - 1, a], rr_ss.at[d, s - 1, a], rr_rs.at[d, s - 1, a])
                total = total + r_recv[d, s - 1, a].astype(F32)
            r_send[d, s, a] = total.astype(BF)
            send(r_send.at[d, s, a], r_recv.at[d, s, a], rr_ss.at[d, s, a], rr_rs.at[d, s, a], ynext[d])

    def rs_last(a):
        h = halves[a]
        total = c_own[h, y]
        for d in range(2):
            s = 3 if a == d else 2
            arrive(r_recv.at[d, s, a], rr_ss.at[d, s, a], rr_rs.at[d, s, a])
            total = total + r_recv[d, s, a].astype(F32)
        hid_all[zl, h, y] = (total * slope[h]).astype(BF)

    def in_z(own, full, ss, rs):
        full[zh % 2, k, my] = own[...]
        for dz in (2, 1, 3):
            send(own, full.at[zh % 2, k, my], ss.at[dz - 1], rs.at[dz - 1], dev(zh=(zh + dz) % 4))

    def in_x(full, zss, zrs, ss, rs):
        for dz in (0, 1, 3, 2):
            zs = (zh + 4 - dz) % 4
            ref = full.at[zs % 2, k, 2 * x + zs // 2]
            if dz > 0:
                arrive(ref, zss.at[dz - 1], zrs.at[dz - 1])
            for dx in (2, 1, 3):
                send(ref, ref, ss.at[dx - 1, dz], rs.at[dx - 1, dz], dev(x=(x + dx) % 4))

    def in_core(full, xss, xrs, ss, rs):
        for dx in (1, 3, 2):
            for dz in range(4):
                xs, zs = (x + 4 - dx) % 4, (zh + 4 - dz) % 4
                arrive(full.at[zs % 2, k, 2 * xs + zs // 2], xss.at[dx - 1, dz], xrs.at[dx - 1, dz])
        for b in range(2):
            send(full.at[b, k], full.at[b, k], ss.at[b], rs.at[b], sib)

    def in_done(full, ss, rs):
        for b in range(2):
            arrive(full.at[b, 1 - k], ss.at[b], rs.at[b])

    partial(0)
    rs_step(0, 0)
    act_step(1, 2)
    act_step(0, 3)
    for dx in (1, 3, 2):
        for zs in range(2):
            ref = og2.at[zs, k, pl.ds(2 * ((x + 4 - dx) % 4), 2)]
            arrive(ref, gs_ss.at[dx - 1, zs], gs_rs.at[dx - 1, zs])
    partial(1)
    rs_step(1, 0)
    send(w_in_hbm, w_in.at[zl], wi_ss, wi_rs, zpart)
    loads[4].wait()
    in_z(og_v, og_all, oz_ss, oz_rs)
    in_z(li_v, li_all, lz_ss, lz_rs)
    act_step(1, 3)
    rs_step(0, 1)
    rs_step(1, 1)
    act_step(0, 4)
    act_step(1, 4)
    in_x(og_all, oz_ss, oz_rs, ox_ss, ox_rs)
    rs_step(0, 2)
    rs_step(1, 2)
    in_x(li_all, lz_ss, lz_rs, lx_ss, lx_rs)
    rs_step(0, 3)
    rs_step(1, 3)
    in_core(og_all, ox_ss, ox_rs, os_ss, os_rs)

    def ag_step(a, s):
        h = halves[a]
        for d in range(2):
            hops = 4 if a == d else 3
            off = (8 - s) % 8 if d == 0 else s
            ref = hid_all.at[zl, h, (y + off) % 8]
            if 0 < s <= hops:
                arrive(ref, hy_ss.at[d, s - 1, a], hy_rs.at[d, s - 1, a])
            if s < hops:
                send(ref, ref, hy_ss.at[d, s, a], hy_rs.at[d, s, a], ynext[d])
            if s <= hops and (s > 0 or d == 0):
                send(ref, ref, hz_ss.at[off, a], hz_rs.at[off, a], zpart)

    def q_part(a, offs):
        at = [(y + o) % 8 for o in offs]
        rows = jnp.concatenate([hid_all[zl, halves[a], p] for p in at], axis=0)
        for zs in range(2):
            q = dot(rows, w_in[zs], 1, 1)
            for i, (o, p) in enumerate(zip(offs, at, strict=True)):
                part = q[i * T : (i + 1) * T]
                if a == 0:
                    q_sib[p, zs] = part
                    if zs == 1:
                        send(q_sib.at[p], q_in.at[p], qs_ss.at[o], qs_rs.at[o], sib)
                    continue
                if zs == 0:
                    arrive(q_in.at[p], qs_ss.at[o], qs_rs.at[o])
                part = part + q_in[p, zs]
                q_send[p, zs] = part.astype(BF)
                mine = (p == my) & same & (zl == zs)

                @pl.when(mine)
                def _():
                    q_self[...] = part

                px, pz = p // 2, 2 * (p % 2) + zl
                slot = (px + 4 - x) % 4 * 4 + (pz + 4 - zh) % 4
                send(q_send.at[p, zs], q_recv.at[slot], q_ss.at[o, zs], q_rs.at[slot], dev(x=px, zh=pz, zl=zs), jnp.logical_not(mine))

    def go_tile(n):
        cols = pl.ds(n * FT, FT)
        go_v[cols, :] = dot(act_all[:, :, :, :, cols].reshape(TOK, FT), og_all[...].reshape(TOK, DB), 0, 0)

    rs_last(0)
    ag_step(0, 0)
    rs_last(1)
    ag_step(1, 0)
    in_core(li_all, lx_ss, lx_rs, ls_ss, ls_rs)
    ag_step(0, 1)
    ag_step(1, 1)
    loads[3].wait()
    arrive(w_in.at[1 - zl], wi_ss, wi_rs)
    q_part(0, (0, 1, 7))
    q_part(1, (0, 1, 7))
    ag_step(0, 2)
    ag_step(1, 2)
    q_part(0, (2, 6))
    q_part(1, (2, 6))
    ag_step(0, 3)
    ag_step(1, 3)
    q_part(0, (3, 5))
    q_part(1, (3, 5))
    ag_step(0, 4)
    q_part(0, (4,))
    ag_step(1, 4)
    q_part(1, (4,))
    in_done(og_all, os_ss, os_rs)
    for n in range(3):
        go_tile(n)
    store_go = pltpu.make_async_copy(go_v, go_out, loc.at[5])
    store_go.start()
    in_done(li_all, ls_ss, ls_rs)
    li_t[...] = li_all[...].reshape(TOK, DB).T
    for o in range(8):
        for a in range(2):
            arrive(hid_all.at[1 - zl, halves[a], (y + o) % 8], hz_ss.at[o, a], hz_rs.at[o, a])
    for n in range(3):
        cols = pl.ds(n * FT, FT)
        gi_v[:, cols] = dot(li_t[...], hid_all[:, :, :, :, cols].reshape(TOK, FT), 1, 0)
    store_gi = pltpu.make_async_copy(gi_v, gi_out, loc.at[6])
    store_gi.start()
    @pl.when(jnp.logical_not(same))
    def _():
        arrive(q_recv.at[0], q_ss.at[0, 0], q_rs.at[0])
        q_self[...] = q_recv[0].astype(F32)

    total = q_self[...]
    for j in range(1, 16):
        arrive(q_recv.at[j], q_ss.at[0, 0], q_rs.at[j])
        total = total + q_recv[j].astype(F32)
    ig_v[...] = total.astype(BF)
    store_ig = pltpu.make_async_copy(ig_v, ig_out, loc.at[7])
    store_ig.start()
    for cond, c in started:
        if cond is None:
            c.wait_send()
        else:
            pl.when(cond)(c.wait_send)
    store_go.wait()
    store_gi.wait()
    store_ig.wait()


def on_device(layer_input, output_grad, preact, weight_in, weight_out):
    hbm = pl.BlockSpec(memory_space=pl.ANY)
    vmem, dma = pltpu.VMEM, pltpu.SemaphoreType.DMA
    sems = [
        ((4,), (2, 4)), ((4, 2, 2), (4, 2, 2)), ((3, 2), (3, 2)),
        ((3,), (3,)), ((3, 4), (3, 4)), ((2,), (2,)), ((3,), (3,)), ((3, 4), (3, 4)), ((2,), (2,)),
        ((2,), (2,)), ((2, 2, 4, 2), (2, 2, 4, 2)), ((2, 4, 2), (2, 4, 2)), ((8, 2), (8, 2)),
        ((3,), (3,)), (None, None), ((2, 4, 2), (2, 4, 2)), ((8,), (8,)), ((8, 2), (16,)),
    ]
    return pl.pallas_call(
        kernel,
        out_shape=(
            jax.ShapeDtypeStruct((T, DB), BF),
            jax.ShapeDtypeStruct((DB, FB), F32),
            jax.ShapeDtypeStruct((FB, DB), F32),
        ),
        in_specs=[hbm] * 5,
        out_specs=(hbm, hbm, hbm),
        scratch_shapes=[
            vmem((T, DB), BF),
            vmem((T, DB), BF),
            vmem((2 * T, FB), BF),
            vmem((T, DB), BF),
            vmem((2, DB, FB), BF),
            vmem((2, FB, DB), BF),
            vmem((2, 2, 8, T, DB), BF),
            vmem((2, 2, 8, T, DB), BF),
            vmem((2, 2, 8, T, DB), BF),
            vmem((2, 2, 8, T, FB), BF),
            vmem((2, 2, 8, T, FB), BF),
            vmem((DB, TOK), BF),
            vmem((2, T, FB), F32),
            vmem((2, 8, T, FB), F32),
            vmem((2, 4, 2, T, FB), BF),
            vmem((2, 4, 2, T, FB), BF),
            vmem((8, 2, T, DB), F32),
            vmem((8, 2, T, DB), F32),
            vmem((8, 2, T, DB), BF),
            vmem((16, T, DB), BF),
            vmem((T, DB), F32),
            vmem((DB, FB), F32),
            vmem((FB, DB), F32),
        ]
        + [dma if s is None else dma(s) for pair in sems for s in pair]
        + [dma((8,))],
        compiler_params=pltpu.CompilerParams(collective_id=0, has_side_effects=True, vmem_limit_bytes=60 * 2**20),
        cost_estimate=pl.CostEstimate(flops=8 * TOK * DB * FB, bytes_accessed=4 * 2**20, transcendentals=2 * 64 * FB),
        name="mlp_backward",
    )(layer_input, output_grad, preact, weight_in, weight_out)


def solution(mesh):
    in_specs = (P("row", "col"), P("row", "col"), P("col", "row"), P("col", "row"), P("row", "col"))
    out_specs = (P("row", "col"), P("col", "row"), P("row", "col"))
    return jax.shard_map(on_device, mesh=mesh, in_specs=in_specs, out_specs=out_specs, check_vma=False)
```

```python
import math

import jax
import jax.numpy as jnp
from jax import lax
from jax.experimental import pallas as pl
from jax.experimental.pallas import tpu as pltpu
from jax.sharding import PartitionSpec as P

MESH = pl.DeviceIdType.MESH
BF, F32 = jnp.bfloat16, jnp.float32
TOK, DB, FB = 1024, 384, 768
T = 32
FT = 256
FA = 512


def gelu_parts(pre):
    cdf = 0.5 * (1.0 + lax.erf(pre * (1.0 / math.sqrt(2.0))))
    pdf = jnp.exp(-0.5 * pre * pre) * (1.0 / math.sqrt(2.0 * math.pi))
    return pre * cdf, cdf + pre * pdf


def dot(a, b, ca, cb):
    return lax.dot_general(a, b, (((ca,), (cb,)), ((), ())), preferred_element_type=F32)


def kernel(
    li, og, pre, w_in_hbm, w_out_hbm, ig_out, gi_out, go_out,
    li_v, og_v, pre_v, w_in, w_out, li_all, og_all, act_all, hid_all, li_t, slope, c_a, c_b, cz_send, cz_recv,
    ra_send, ra_recv, rb_send, rb_recv, bz_send, bz_recv, q_sib, q_in, q_send, q_recv, q_self,
    oz_ss, oz_rs, ox_ss, ox_rs, os_ss, os_rs, lz_ss, lz_rs, lx_ss, lx_rs, ls_ss, ls_rs,
    az_ss, az_rs, ay_ss, ay_rs, hy_ss, hy_rs, hz_ss, hz_rs, wi_ss, wi_rs, cz_ss, cz_rs, ra_ss, ra_rs, rb_ss, rb_rs, bz_ss, bz_rs,
    qs_ss, qs_rs, q_ss, q_rs, loc,
):
    row, col = lax.axis_index("row"), lax.axis_index("col")
    x, zh, k = row // 8, (row // 2) % 4, row % 2
    y, zl = col // 2, col % 2
    halves = (1 - k, k)
    my = 2 * x + zh // 2
    same = zh % 2 == zl

    def dev(x=x, zh=zh, k=k, y=y, zl=zl):
        return (x * 8 + zh * 2 + k, y * 2 + zl)

    sib, zpart = dev(k=1 - k), dev(zl=1 - zl)
    ynext = [dev(y=(y + 1) % 8), dev(y=(y + 7) % 8)]
    started = []

    def send(src, dst, ss, rs, to, cond=None):
        c = pltpu.make_async_remote_copy(src_ref=src, dst_ref=dst, send_sem=ss, recv_sem=rs, device_id=to, device_id_type=MESH)
        if cond is None:
            c.start()
        else:
            pl.when(cond)(c.start)
        started.append((cond, c))

    def arrive(dst, ss, rs):
        pltpu.make_async_remote_copy(src_ref=dst, dst_ref=dst, send_sem=ss, recv_sem=rs, device_id=sib, device_id_type=MESH).wait_recv()

    loads = [
        pltpu.make_async_copy(a, b, loc.at[i])
        for i, (a, b) in enumerate([(og, og_v), (pre, pre_v), (w_out_hbm, w_out), (w_in_hbm, w_in.at[zl]), (li, li_v)])
    ]
    for c in loads:
        c.start()

    barrier = pltpu.get_barrier_semaphore()
    greet = [dev(zh=(zh + a) % 4, zl=(zl + b) % 2) for a in range(4) for b in range(2) if (a, b) != (0, 0)]
    greet += [dev(x=(x + a) % 4, k=c) for a in (1, 2, 3) for c in (k, 1 - k)] + ynext + [sib]
    greet += [dev(x=(x + a) % 4, zh=b, zl=zh % 2) for a in (1, 2, 3) for b in range(4)]
    for p in greet:
        pl.semaphore_signal(barrier, inc=1, device_id=p, device_id_type=MESH)
    loads[0].wait()
    pl.semaphore_wait(barrier, len(greet))

    def in_z(own, full, ss, rs):
        full[zh % 2, k, my] = own[...]
        for dz in (2, 1, 3):
            send(own, full.at[zh % 2, k, my], ss.at[dz - 1], rs.at[dz - 1], dev(zh=(zh + dz) % 4))

    def in_x(full, zss, zrs, ss, rs):
        for dz in (0, 1, 3, 2):
            zs = (zh + 4 - dz) % 4
            ref = full.at[zs % 2, k, 2 * x + zs // 2]
            if dz > 0:
                arrive(ref, zss.at[dz - 1], zrs.at[dz - 1])
            for dx in (2, 1, 3, 0):
                send(ref, ref, ss.at[dx, dz], rs.at[dx, dz], dev(x=(x + dx) % 4, k=1 - k))

    def in_core(full, xss, xrs, ss, rs):
        for dx in (0, 1, 3, 2):
            xs = (x + 4 - dx) % 4
            for dz in range(4):
                zs = (zh + 4 - dz) % 4
                arrive(full.at[zs % 2, 1 - k, 2 * xs + zs // 2], xss.at[dx, dz], xrs.at[dx, dz])
            if dx > 0:
                for b in range(2):
                    ref = full.at[b, 1 - k, pl.ds(2 * xs, 2)]
                    send(ref, ref, ss.at[dx - 1, b], rs.at[dx - 1, b], sib)

    def in_done(full, ss, rs):
        for dx in (1, 3, 2):
            for b in range(2):
                arrive(full.at[b, k, pl.ds(2 * ((x + 4 - dx) % 4), 2)], ss.at[dx - 1, b], rs.at[dx - 1, b])

    in_z(og_v, og_all, oz_ss, oz_rs)
    loads[1].wait()
    for h in range(2):
        value, sl = gelu_parts(pre_v[pl.ds(h * T, T), :].astype(F32))
        act_all[zl, h, y] = value.astype(BF)
        slope[h] = sl

    def act_step(j, s):
        zz = zl if j == 0 else 1 - zl
        for h in range(2):
            if s == 0 and j == 0:
                ref = act_all.at[zl, h, y]
                send(ref, ref, az_ss.at[h], az_rs.at[h], zpart)
            if s == 0 and j == 1:
                arrive(act_all.at[zz, h, y], az_ss.at[h], az_rs.at[h])
            for d in range(2):
                hops = 4 if h == d else 3
                ref = act_all.at[zz, h, (y + (8 - s if d == 0 else s)) % 8]
                if 0 < s <= hops:
                    arrive(ref, ay_ss.at[j, d, s - 1, h], ay_rs.at[j, d, s - 1, h])
                if s < hops:
                    send(ref, ref, ay_ss.at[j, d, s, h], ay_rs.at[j, d, s, h], ynext[d])

    act_step(0, 0)
    in_x(og_all, oz_ss, oz_rs, ox_ss, ox_rs)
    send(w_in_hbm, w_in.at[zl], wi_ss, wi_rs, zpart)
    act_step(0, 1)
    in_core(og_all, ox_ss, ox_rs, os_ss, os_rs)
    act_step(1, 0)

    def partial(half, a, n):
        return dot(og_all[half, halves[a]].reshape(8 * T, DB), w_out[pl.ds(n * FT, FT), :], 1, 1).reshape(8, T, FT)

    def partials(a):
        h = halves[a]
        for n in (1, 2):
            cz_send[h, :, :, pl.ds(n * FT - FT, FT)] = partial(1 - zl, a, n).astype(BF)
        for o in (4, 3, 5, 2, 6, 1, 7, 0):
            at = (y + o) % 8
            send(cz_send.at[h, at], cz_recv.at[h, at], cz_ss.at[o, a], cz_rs.at[o, a], zpart)
        for b in range(2):
            c_b[h, :, b] = partial(b, a, 0)
        rs_b(a, 0)
        for n in (1, 2):
            c_a[h, :, :, pl.ds(n * FT - FT, FT)] = partial(zl, a, n)

    def rs_b(a, s):
        h = halves[a]
        for d in range(2):
            hops = 3 if a == d else 4
            if s >= hops:
                continue
            to = hops - s
            total = c_b[h, (y + (to if d == 0 else 8 - to)) % 8]
            if s > 0:
                arrive(rb_recv.at[d, s - 1, a], rb_ss.at[d, s - 1, a], rb_rs.at[d, s - 1, a])
                total = total + rb_recv[d, s - 1, a].astype(F32)
            rb_send[d, s, a] = total.astype(BF)
            send(rb_send.at[d, s, a], rb_recv.at[d, s, a], rb_ss.at[d, s, a], rb_rs.at[d, s, a], ynext[d])

    def mine(a, o):
        h, at = halves[a], (y + o) % 8
        arrive(cz_recv.at[h, at], cz_ss.at[o, a], cz_rs.at[o, a])
        return c_a[h, at] + cz_recv[h, at].astype(F32)

    def rs_a(a, s):
        for d in range(2):
            hops = 4 if a == d else 3
            if s >= hops:
                continue
            to = hops - s
            total = mine(a, to if d == 0 else 8 - to)
            if s > 0:
                arrive(ra_recv.at[d, s - 1, a], ra_ss.at[d, s - 1, a], ra_rs.at[d, s - 1, a])
                total = total + ra_recv[d, s - 1, a].astype(F32)
            ra_send[d, s, a] = total.astype(BF)
            send(ra_send.at[d, s, a], ra_recv.at[d, s, a], ra_ss.at[d, s, a], ra_rs.at[d, s, a], ynext[d])

    def last_b(a):
        h = halves[a]
        for d in range(2):
            s = 2 if a == d else 3
            arrive(rb_recv.at[d, s, a], rb_ss.at[d, s, a], rb_rs.at[d, s, a])
        bz_send[a] = (c_b[h, y, 1 - zl] + rb_recv[0, 2 if a == 0 else 3, a, 1 - zl].astype(F32) + rb_recv[1, 2 if a == 1 else 3, a, 1 - zl].astype(F32)).astype(BF)
        send(bz_send.at[a], bz_recv.at[a], bz_ss.at[a], bz_rs.at[a], zpart)

    def last_a(a):
        h = halves[a]
        total = mine(a, 0)
        for d in range(2):
            s = 3 if a == d else 2
            arrive(ra_recv.at[d, s, a], ra_ss.at[d, s, a], ra_rs.at[d, s, a])
            total = total + ra_recv[d, s, a].astype(F32)
        hid_all[zl, h, y, :, pl.ds(FT, FA)] = (total * slope[h, :, pl.ds(FT, FA)]).astype(BF)
        total = c_b[h, y, zl] + rb_recv[0, 2 if a == 0 else 3, a, zl].astype(F32) + rb_recv[1, 2 if a == 1 else 3, a, zl].astype(F32)
        arrive(bz_recv.at[a], bz_ss.at[a], bz_rs.at[a])
        total = total + bz_recv[a].astype(F32)
        hid_all[zl, h, y, :, pl.ds(0, FT)] = (total * slope[h, :, pl.ds(0, FT)]).astype(BF)

    loads[2].wait()
    partials(0)
    act_step(1, 1)
    in_done(og_all, os_ss, os_rs)
    partials(1)
    rs_a(0, 0)
    rs_a(1, 0)
    act_step(0, 2)
    rs_b(0, 1)
    rs_b(1, 1)
    rs_a(0, 1)
    rs_a(1, 1)
    act_step(1, 2)
    rs_b(0, 2)
    rs_b(1, 2)
    rs_a(0, 2)
    rs_a(1, 2)
    rs_b(0, 3)
    rs_b(1, 3)
    rs_a(0, 3)
    rs_a(1, 3)
    act_step(0, 3)
    loads[4].wait()
    in_z(li_v, li_all, lz_ss, lz_rs)
    last_b(0)
    last_b(1)

    def ag_step(a, s):
        h = halves[a]
        for d in range(2):
            hops = 4 if a == d else 3
            off = (8 - s) % 8 if d == 0 else s
            ref = hid_all.at[zl, h, (y + off) % 8]
            if 0 < s <= hops:
                arrive(ref, hy_ss.at[d, s - 1, a], hy_rs.at[d, s - 1, a])
            if s < hops:
                send(ref, ref, hy_ss.at[d, s, a], hy_rs.at[d, s, a], ynext[d])
            if s <= hops and (s > 0 or d == 0):
                send(ref, ref, hz_ss.at[off, a], hz_rs.at[off, a], zpart)

    def q_part(a, offs):
        at = [(y + o) % 8 for o in offs]
        rows = jnp.concatenate([hid_all[zl, halves[a], p] for p in at], axis=0)
        for zs in range(2):
            q = dot(rows, w_in[zs], 1, 1)
            for i, (o, p) in enumerate(zip(offs, at, strict=True)):
                part = q[i * T : (i + 1) * T]
                if a == 0:
                    q_sib[p, zs] = part
                    if zs == 1:
                        send(q_sib.at[p], q_in.at[p], qs_ss.at[o], qs_rs.at[o], sib)
                    continue
                if zs == 0:
                    arrive(q_in.at[p], qs_ss.at[o], qs_rs.at[o])
                part = part + q_in[p, zs]
                q_send[p, zs] = part.astype(BF)
                stays = (p == my) & same & (zl == zs)

                @pl.when(stays)
                def _():
                    q_self[...] = part

                px, pz = p // 2, 2 * (p % 2) + zl
                slot = (px + 4 - x) % 4 * 4 + (pz + 4 - zh) % 4
                send(q_send.at[p, zs], q_recv.at[slot], q_ss.at[o, zs], q_rs.at[slot], dev(x=px, zh=pz, zl=zs), jnp.logical_not(stays))

    def go_tile(n):
        cols = pl.ds(n * FT, FT)
        go_out[cols, :] = dot(act_all[:, :, :, :, cols].reshape(TOK, FT), og_all[...].reshape(TOK, DB), 0, 0)

    last_a(0)
    ag_step(0, 0)
    last_a(1)
    ag_step(1, 0)
    act_step(1, 3)
    act_step(0, 4)
    in_x(li_all, lz_ss, lz_rs, lx_ss, lx_rs)
    ag_step(0, 1)
    ag_step(1, 1)
    loads[3].wait()
    arrive(w_in.at[1 - zl], wi_ss, wi_rs)
    q_part(0, (0, 1, 7))
    q_part(1, (0, 1, 7))
    act_step(1, 4)
    ag_step(0, 2)
    ag_step(1, 2)
    q_part(0, (2, 6))
    q_part(1, (2, 6))
    in_core(li_all, lx_ss, lx_rs, ls_ss, ls_rs)
    ag_step(0, 3)
    ag_step(1, 3)
    q_part(0, (3, 5))
    q_part(1, (3, 5))
    ag_step(0, 4)
    q_part(0, (4,))
    ag_step(1, 4)
    q_part(1, (4,))
    for n in range(3):
        go_tile(n)
    in_done(li_all, ls_ss, ls_rs)
    li_t[...] = li_all[...].reshape(TOK, DB).T
    for o in range(8):
        for a in range(2):
            arrive(hid_all.at[1 - zl, halves[a], (y + o) % 8], hz_ss.at[o, a], hz_rs.at[o, a])
    for n in range(3):
        cols = pl.ds(n * FT, FT)
        gi_out[:, cols] = dot(li_t[...], hid_all[:, :, :, :, cols].reshape(TOK, FT), 1, 0)
    @pl.when(jnp.logical_not(same))
    def _():
        arrive(q_recv.at[0], q_ss.at[0, 0], q_rs.at[0])
        q_self[...] = q_recv[0].astype(F32)

    total = q_self[...]
    for j in range(1, 16):
        arrive(q_recv.at[j], q_ss.at[0, 0], q_rs.at[j])
        total = total + q_recv[j].astype(F32)
    ig_out[...] = total.astype(BF)
    for cond, c in started:
        if cond is None:
            c.wait_send()
        else:
            pl.when(cond)(c.wait_send)


def on_device(layer_input, output_grad, preact, weight_in, weight_out):
    vmem, dma = pltpu.VMEM, pltpu.SemaphoreType.DMA
    ins = [pltpu.with_memory_space_constraint(a, pltpu.HBM) for a in (layer_input, output_grad, preact, weight_in, weight_out)]
    gather = [(3,), (3,), (4, 4), (4, 4), (3, 2), (3, 2)]
    sems = gather + gather
    sems += [s for s in [(2,), (2, 2, 4, 2), (2, 4, 2), (8, 2), None, (8, 2), (2, 4, 2), (2, 4, 2), (2,), (8,)] for _ in range(2)]
    sems += [(8, 2), (16,), (5,)]
    return pl.pallas_call(
        kernel,
        out_shape=(
            jax.ShapeDtypeStruct((T, DB), BF),
            jax.ShapeDtypeStruct((DB, FB), F32),
            jax.ShapeDtypeStruct((FB, DB), F32),
        ),
        in_specs=[pl.BlockSpec(memory_space=pltpu.HBM)] * 5,
        out_specs=(pl.BlockSpec(memory_space=pltpu.VMEM),) * 3,
        scratch_shapes=[
            vmem((T, DB), BF),
            vmem((T, DB), BF),
            vmem((2 * T, FB), BF),
            vmem((2, DB, FB), BF),
            vmem((FB, DB), BF),
            vmem((2, 2, 8, T, DB), BF),
            vmem((2, 2, 8, T, DB), BF),
            vmem((2, 2, 8, T, FB), BF),
            vmem((2, 2, 8, T, FB), BF),
            vmem((DB, TOK), BF),
            vmem((2, T, FB), F32),
            vmem((2, 8, T, FA), F32),
            vmem((2, 8, 2, T, FT), F32),
            vmem((2, 8, T, FA), BF),
            vmem((2, 8, T, FA), BF),
            vmem((2, 4, 2, T, FA), BF),
            vmem((2, 4, 2, T, FA), BF),
            vmem((2, 4, 2, 2, T, FT), BF),
            vmem((2, 4, 2, 2, T, FT), BF),
            vmem((2, T, FT), BF),
            vmem((2, T, FT), BF),
            vmem((8, 2, T, DB), F32),
            vmem((8, 2, T, DB), F32),
            vmem((8, 2, T, DB), BF),
            vmem((16, T, DB), BF),
            vmem((T, DB), F32),
        ]
        + [dma if s is None else dma(s) for s in sems],
        compiler_params=pltpu.CompilerParams(collective_id=0, has_side_effects=True, vmem_limit_bytes=48 * 2**20),
        cost_estimate=pl.CostEstimate(flops=8 * TOK * DB * FB, bytes_accessed=4 * 2**20, transcendentals=2 * 64 * FB),
        name="mlp_backward",
    )(*ins)


def solution(mesh):
    in_specs = (P("row", "col"), P("row", "col"), P("col", "row"), P("col", "row"), P("row", "col"))
    out_specs = (P("row", "col"), P("col", "row"), P("row", "col"))
    return jax.shard_map(on_device, mesh=mesh, in_specs=in_specs, out_specs=out_specs, check_vma=False)
```

```python
import math

import jax
import jax.numpy as jnp
from jax import lax
from jax.experimental import pallas as pl
from jax.experimental.pallas import tpu as pltpu
from jax.sharding import PartitionSpec as P

MESH = pl.DeviceIdType.MESH
BF, F32 = jnp.bfloat16, jnp.float32
TOK, DB, FB = 1024, 384, 768
T = 32
FT = 256
FA = 512


def gelu_parts(pre):
    cdf = 0.5 * (1.0 + lax.erf(pre * (1.0 / math.sqrt(2.0))))
    pdf = jnp.exp(-0.5 * pre * pre) * (1.0 / math.sqrt(2.0 * math.pi))
    return pre * cdf, cdf + pre * pdf


def dot(a, b, ca, cb):
    return lax.dot_general(a, b, (((ca,), (cb,)), ((), ())), preferred_element_type=F32)


def kernel(
    li, og, pre, w_in_hbm, w_out_hbm, ig_out, gi_out, go_out,
    li_v, og_v, pre_v, w_in, w_out, li_all, og_all, act_all, hid_all, li_t, slope, c_a, c_b, cz_send, cz_recv,
    ra_send, ra_recv, rb_send, rb_recv, bz_send, bz_recv, q_sib, q_in, q_send, q_recv, q_self,
    oz_ss, oz_rs, ox_ss, ox_rs, os_ss, os_rs, lz_ss, lz_rs, lx_ss, lx_rs, ls_ss, ls_rs,
    az_ss, az_rs, ay_ss, ay_rs, hy_ss, hy_rs, hz_ss, hz_rs, cz_ss, cz_rs, ra_ss, ra_rs, rb_ss, rb_rs, bz_ss, bz_rs,
    qs_ss, qs_rs, q_ss, q_rs, loc,
):
    row, col = lax.axis_index("row"), lax.axis_index("col")
    x, zh, k = row // 8, (row // 2) % 4, row % 2
    y, zl = col // 2, col % 2
    halves = (1 - k, k)
    my = 4 * x + zh

    def dev(x=x, zh=zh, k=k, y=y, zl=zl):
        return (x * 8 + zh * 2 + k, y * 2 + zl)

    sib, zpart = dev(k=1 - k), dev(zl=1 - zl)
    ynext = [dev(y=(y + 1) % 8), dev(y=(y + 7) % 8)]
    started = []

    def send(src, dst, ss, rs, to, cond=None):
        c = pltpu.make_async_remote_copy(src_ref=src, dst_ref=dst, send_sem=ss, recv_sem=rs, device_id=to, device_id_type=MESH)
        if cond is None:
            c.start()
        else:
            pl.when(cond)(c.start)
        started.append((cond, c))

    def arrive(dst, ss, rs):
        pltpu.make_async_remote_copy(src_ref=dst, dst_ref=dst, send_sem=ss, recv_sem=rs, device_id=sib, device_id_type=MESH).wait_recv()

    loads = [
        pltpu.make_async_copy(a, b, loc.at[i])
        for i, (a, b) in enumerate([(og, og_v), (pre, pre_v), (w_out_hbm, w_out), (w_in_hbm, w_in), (li, li_v)])
    ]
    for c in loads:
        c.start()

    barrier = pltpu.get_barrier_semaphore()
    greet = [dev(x=(x + a) % 4, zh=(zh + b) % 4) for a in range(4) for b in range(4) if (a, b) != (0, 0)]
    greet += [dev(x=(x + a) % 4, k=1 - k) for a in (1, 2, 3)] + ynext + [sib, zpart]
    for p in greet:
        pl.semaphore_signal(barrier, inc=1, device_id=p, device_id_type=MESH)
    loads[0].wait()
    pl.semaphore_wait(barrier, len(greet))

    def in_z(own, full, ss, rs):
        full[k, my] = own[...]
        for dz in (2, 1, 3):
            send(own, full.at[k, my], ss.at[dz - 1], rs.at[dz - 1], dev(zh=(zh + dz) % 4))

    def in_x(full, zss, zrs, ss, rs):
        for dz in (0, 1, 3, 2):
            ref = full.at[k, 4 * x + (zh + 4 - dz) % 4]
            if dz > 0:
                arrive(ref, zss.at[dz - 1], zrs.at[dz - 1])
            for dx in (2, 1, 3, 0):
                send(ref, ref, ss.at[dx, dz], rs.at[dx, dz], dev(x=(x + dx) % 4, k=1 - k))

    def in_core(full, xss, xrs, ss, rs):
        for dx in (0, 1, 3, 2):
            xs = (x + 4 - dx) % 4
            for dz in range(4):
                arrive(full.at[1 - k, 4 * xs + (zh + 4 - dz) % 4], xss.at[dx, dz], xrs.at[dx, dz])
            if dx > 0:
                ref = full.at[1 - k, pl.ds(4 * xs, 4)]
                send(ref, ref, ss.at[dx - 1], rs.at[dx - 1], sib)

    def in_done(full, ss, rs):
        for dx in (1, 3, 2):
            arrive(full.at[k, pl.ds(4 * ((x + 4 - dx) % 4), 4)], ss.at[dx - 1], rs.at[dx - 1])

    def swap(full, a, ss, rs):
        ref = full.at[halves[a], col]
        send(ref, ref, ss.at[a], rs.at[a], zpart)

    def ring(full, j, s, a, zss, zrs, ss, rs):
        zz = zl if j == 0 else 1 - zl
        if j == 1 and s == 0:
            arrive(full.at[halves[a], 2 * y + zz], zss.at[a], zrs.at[a])
        for d in range(2):
            hops = 4 if a == d else 3
            ref = full.at[halves[a], 2 * ((y + (8 - s if d == 0 else s)) % 8) + zz]
            if 0 < s <= hops:
                arrive(ref, ss.at[j, d, s - 1, a], rs.at[j, d, s - 1, a])
            if s < hops:
                send(ref, ref, ss.at[j, d, s, a], rs.at[j, d, s, a], ynext[d])

    in_z(og_v, og_all, oz_ss, oz_rs)
    loads[1].wait()
    for h in range(2):
        value, sl = gelu_parts(pre_v[pl.ds(h * T, T), :].astype(F32))
        act_all[h, col] = value.astype(BF)
        slope[h] = sl

    def act_step(j, s):
        for a in range(2):
            if j == 0 and s == 0:
                swap(act_all, a, az_ss, az_rs)
            ring(act_all, j, s, a, az_ss, az_rs, ay_ss, ay_rs)

    def hid_step(j, s, a):
        ring(hid_all, j, s, a, hz_ss, hz_rs, hy_ss, hy_rs)

    act_step(0, 0)
    act_step(0, 1)
    act_step(1, 0)
    in_x(og_all, oz_ss, oz_rs, ox_ss, ox_rs)
    act_step(1, 1)
    act_step(0, 2)
    loads[4].wait()
    in_core(og_all, ox_ss, ox_rs, os_ss, os_rs)

    def partial(a, n):
        return dot(og_all[halves[a]].reshape(16 * T, DB), w_out[pl.ds(n * FT, FT), :], 1, 1).reshape(8, 2, T, FT)

    def partials(a):
        h = halves[a]
        for n in (1, 2):
            c_a[h, :, :, :, pl.ds(n * FT - FT, FT)] = partial(a, n)
        for o in (4, 3, 5, 2, 6, 1, 7, 0):
            at = (y + o) % 8
            cz_send[h, at] = c_a[h, at, 1 - zl].astype(BF)
            send(cz_send.at[h, at], cz_recv.at[h, at], cz_ss.at[o, a], cz_rs.at[o, a], zpart)
        c_b[h] = partial(a, 0)
        rs_b(a, 0)

    def rs_b(a, s):
        h = halves[a]
        for d in range(2):
            hops = 3 if a == d else 4
            if s >= hops:
                continue
            to = hops - s
            total = c_b[h, (y + (to if d == 0 else 8 - to)) % 8]
            if s > 0:
                arrive(rb_recv.at[d, s - 1, a], rb_ss.at[d, s - 1, a], rb_rs.at[d, s - 1, a])
                total = total + rb_recv[d, s - 1, a].astype(F32)
            rb_send[d, s, a] = total.astype(BF)
            send(rb_send.at[d, s, a], rb_recv.at[d, s, a], rb_ss.at[d, s, a], rb_rs.at[d, s, a], ynext[d])

    def mine(a, o):
        h, at = halves[a], (y + o) % 8
        arrive(cz_recv.at[h, at], cz_ss.at[o, a], cz_rs.at[o, a])
        return c_a[h, at, zl] + cz_recv[h, at].astype(F32)

    def rs_a(a, s):
        for d in range(2):
            hops = 4 if a == d else 3
            if s >= hops:
                continue
            to = hops - s
            total = mine(a, to if d == 0 else 8 - to)
            if s > 0:
                arrive(ra_recv.at[d, s - 1, a], ra_ss.at[d, s - 1, a], ra_rs.at[d, s - 1, a])
                total = total + ra_recv[d, s - 1, a].astype(F32)
            ra_send[d, s, a] = total.astype(BF)
            send(ra_send.at[d, s, a], ra_recv.at[d, s, a], ra_ss.at[d, s, a], ra_rs.at[d, s, a], ynext[d])

    def last_b(a):
        h = halves[a]
        for d in range(2):
            s = 2 if a == d else 3
            arrive(rb_recv.at[d, s, a], rb_ss.at[d, s, a], rb_rs.at[d, s, a])
        bz_send[a] = (c_b[h, y, 1 - zl] + rb_recv[0, 2 if a == 0 else 3, a, 1 - zl].astype(F32) + rb_recv[1, 2 if a == 1 else 3, a, 1 - zl].astype(F32)).astype(BF)
        send(bz_send.at[a], bz_recv.at[a], bz_ss.at[a], bz_rs.at[a], zpart)

    def last_a(a):
        h = halves[a]
        total = mine(a, 0)
        for d in range(2):
            s = 3 if a == d else 2
            arrive(ra_recv.at[d, s, a], ra_ss.at[d, s, a], ra_rs.at[d, s, a])
            total = total + ra_recv[d, s, a].astype(F32)
        hid_all[h, col, :, pl.ds(FT, FA)] = (total * slope[h, :, pl.ds(FT, FA)]).astype(BF)
        total = c_b[h, y, zl] + rb_recv[0, 2 if a == 0 else 3, a, zl].astype(F32) + rb_recv[1, 2 if a == 1 else 3, a, zl].astype(F32)
        arrive(bz_recv.at[a], bz_ss.at[a], bz_rs.at[a])
        total = total + bz_recv[a].astype(F32)
        hid_all[h, col, :, pl.ds(0, FT)] = (total * slope[h, :, pl.ds(0, FT)]).astype(BF)

    loads[2].wait()
    partials(0)
    in_done(og_all, os_ss, os_rs)
    partials(1)
    act_step(1, 2)
    act_step(0, 3)
    in_z(li_v, li_all, lz_ss, lz_rs)
    rs_a(0, 0)
    rs_a(1, 0)
    rs_b(0, 1)
    rs_b(1, 1)
    rs_a(0, 1)
    rs_a(1, 1)
    act_step(1, 3)
    rs_b(0, 2)
    rs_b(1, 2)
    rs_a(0, 2)
    rs_a(1, 2)
    rs_b(0, 3)
    rs_b(1, 3)
    rs_a(0, 3)
    rs_a(1, 3)
    in_x(li_all, lz_ss, lz_rs, lx_ss, lx_rs)
    last_b(0)
    last_b(1)

    def q_part(a, offs):
        h = halves[a]
        at = [2 * ((y + o) % 8) for o in offs]
        rows = jnp.concatenate([hid_all[h, pl.ds(p, 2)].reshape(2 * T, FB) for p in at], axis=0)
        q = dot(rows, w_in[...], 1, 1)
        for i, (o, p) in enumerate(zip(offs, at, strict=True)):
            part = q[2 * i * T : 2 * (i + 1) * T].reshape(2, T, DB)
            if a == 0:
                q_sib[pl.ds(p, 2)] = part
                send(q_sib.at[pl.ds(p, 2)], q_in.at[pl.ds(p, 2)], qs_ss.at[o], qs_rs.at[o], sib)
                continue
            arrive(q_in.at[pl.ds(p, 2)], qs_ss.at[o], qs_rs.at[o])
            part = part + q_in[pl.ds(p, 2)]
            q_send[pl.ds(p, 2)] = part.astype(BF)
            for b in range(2):
                stays = p + b == my

                @pl.when(stays)
                def _():
                    q_self[...] = part[b]

                px, pz = (p + b) // 4, (p + b) % 4
                slot = (px + 4 - x) % 4 * 4 + (pz + 4 - zh) % 4
                send(q_send.at[p + b], q_recv.at[slot], q_ss.at[o, b], q_rs.at[slot], dev(x=px, zh=pz), jnp.logical_not(stays))

    def go_tile(n):
        cols = pl.ds(n * FT, FT)
        go_out[cols, :] = dot(act_all[:, :, :, cols].reshape(TOK, FT), og_all[...].reshape(TOK, DB), 0, 0)

    for a in range(2):
        last_a(a)
        swap(hid_all, a, hz_ss, hz_rs)
        hid_step(0, 0, a)
    act_step(0, 4)
    act_step(1, 4)
    go_tile(0)
    hid_step(1, 0, 0)
    hid_step(1, 0, 1)
    for j in range(2):
        hid_step(j, 1, 0)
        hid_step(j, 1, 1)
    go_tile(1)
    in_core(li_all, lx_ss, lx_rs, ls_ss, ls_rs)
    loads[3].wait()
    for j in range(2):
        hid_step(j, 2, 0)
        hid_step(j, 2, 1)
    q_part(0, (0, 1, 7, 2, 6))
    for j in range(2):
        hid_step(j, 3, 0)
        hid_step(j, 3, 1)
    q_part(1, (0, 1, 7, 2, 6))
    q_part(0, (3, 5))
    hid_step(0, 4, 0)
    hid_step(0, 4, 1)
    q_part(1, (3, 5))
    hid_step(1, 4, 0)
    q_part(0, (4,))
    hid_step(1, 4, 1)
    q_part(1, (4,))
    go_tile(2)
    in_done(li_all, ls_ss, ls_rs)
    li_t[...] = li_all[...].reshape(TOK, DB).T
    for n in range(3):
        cols = pl.ds(n * FT, FT)
        gi_out[:, cols] = dot(li_t[...], hid_all[:, :, :, cols].reshape(TOK, FT), 1, 0)
    total = q_self[...]
    for j in range(1, 16):
        arrive(q_recv.at[j], q_ss.at[0, 0], q_rs.at[j])
        total = total + q_recv[j].astype(F32)
    ig_out[...] = total.astype(BF)
    for cond, c in started:
        if cond is None:
            c.wait_send()
        else:
            pl.when(cond)(c.wait_send)


def on_device(layer_input, output_grad, preact, weight_in, weight_out):
    vmem, dma = pltpu.VMEM, pltpu.SemaphoreType.DMA
    ins = [pltpu.with_memory_space_constraint(a, pltpu.HBM) for a in (layer_input, output_grad, preact, weight_in, weight_out)]
    gather = [(3,), (3,), (4, 4), (4, 4), (3,), (3,)]
    sems = gather + gather
    sems += [s for s in [(2,), (2, 2, 4, 2), (2, 2, 4, 2), (2,), (8, 2), (2, 4, 2), (2, 4, 2), (2,), (8,)] for _ in range(2)]
    sems += [(8, 2), (16,), (5,)]
    return pl.pallas_call(
        kernel,
        out_shape=(
            jax.ShapeDtypeStruct((T, DB), BF),
            jax.ShapeDtypeStruct((DB, FB), F32),
            jax.ShapeDtypeStruct((FB, DB), F32),
        ),
        in_specs=[pl.BlockSpec(memory_space=pltpu.HBM)] * 5,
        out_specs=(pl.BlockSpec(memory_space=pltpu.VMEM),) * 3,
        scratch_shapes=[
            vmem((T, DB), BF),
            vmem((T, DB), BF),
            vmem((2 * T, FB), BF),
            vmem((DB, FB), BF),
            vmem((FB, DB), BF),
            vmem((2, 16, T, DB), BF),
            vmem((2, 16, T, DB), BF),
            vmem((2, 16, T, FB), BF),
            vmem((2, 16, T, FB), BF),
            vmem((DB, TOK), BF),
            vmem((2, T, FB), F32),
            vmem((2, 8, 2, T, FA), F32),
            vmem((2, 8, 2, T, FT), F32),
            vmem((2, 8, T, FA), BF),
            vmem((2, 8, T, FA), BF),
            vmem((2, 4, 2, T, FA), BF),
            vmem((2, 4, 2, T, FA), BF),
            vmem((2, 4, 2, 2, T, FT), BF),
            vmem((2, 4, 2, 2, T, FT), BF),
            vmem((2, T, FT), BF),
            vmem((2, T, FT), BF),
            vmem((16, T, DB), F32),
            vmem((16, T, DB), F32),
            vmem((16, T, DB), BF),
            vmem((16, T, DB), BF),
            vmem((T, DB), F32),
        ]
        + [dma(s) for s in sems],
        compiler_params=pltpu.CompilerParams(collective_id=0, has_side_effects=True, vmem_limit_bytes=48 * 2**20),
        cost_estimate=pl.CostEstimate(flops=8 * TOK * DB * FB, bytes_accessed=4 * 2**20, transcendentals=2 * 64 * FB),
        name="mlp_backward",
    )(*ins)


def solution(mesh):
    in_specs = (P("row", "col"), P("row", "col"), P("col", "row"), P("col", "row"), P("row", "col"))
    out_specs = (P("row", "col"), P("col", "row"), P("row", "col"))
    return jax.shard_map(on_device, mesh=mesh, in_specs=in_specs, out_specs=out_specs, check_vma=False)
```

```python
import math

import jax
import jax.numpy as jnp
from jax import lax
from jax.experimental import pallas as pl
from jax.experimental.pallas import tpu as pltpu
from jax.sharding import PartitionSpec as P

MESH = pl.DeviceIdType.MESH
BF, F32 = jnp.bfloat16, jnp.float32
TOK, DB, FB = 1024, 384, 768
T = 32
FT = 256
FA = 512


def gelu_parts(pre):
    cdf = 0.5 * (1.0 + lax.erf(pre * (1.0 / math.sqrt(2.0))))
    pdf = jnp.exp(-0.5 * pre * pre) * (1.0 / math.sqrt(2.0 * math.pi))
    return pre * cdf, cdf + pre * pdf


def dot(a, b, ca, cb):
    return lax.dot_general(a, b, (((ca,), (cb,)), ((), ())), preferred_element_type=F32)


def kernel(
    li, og, pre, w_in_hbm, w_out_hbm, ig_out, gi_out, go_out,
    li_v, og_v, pre_v, w_in, w_out, li_all, og_all, act_all, hid_all, li_t, slope, c_a, c_b, cz_send, cz_recv,
    ra_send, ra_recv, rb_send, rb_recv, bz_send, bz_recv, q_sib, q_in, q_send, q_recv, q_self,
    oz_ss, oz_rs, ox_ss, ox_rs, os_ss, os_rs, lz_ss, lz_rs, lx_ss, lx_rs, ls_ss, ls_rs,
    az_ss, az_rs, ay_ss, ay_rs, hy_ss, hy_rs, hz_ss, hz_rs, cz_ss, cz_rs, ra_ss, ra_rs, rb_ss, rb_rs, bz_ss, bz_rs,
    qs_ss, qs_rs, q_ss, q_rs, loc,
):
    row, col = lax.axis_index("row"), lax.axis_index("col")
    x, zh, k = row // 8, (row // 2) % 4, row % 2
    y, zl = col // 2, col % 2
    halves = (1 - k, k)
    my = 4 * x + zh

    def dev(x=x, zh=zh, k=k, y=y, zl=zl):
        return (x * 8 + zh * 2 + k, y * 2 + zl)

    sib, zpart = dev(k=1 - k), dev(zl=1 - zl)
    ynext = [dev(y=(y + 1) % 8), dev(y=(y + 7) % 8)]
    started = []

    def send(src, dst, ss, rs, to, cond=None):
        c = pltpu.make_async_remote_copy(src_ref=src, dst_ref=dst, send_sem=ss, recv_sem=rs, device_id=to, device_id_type=MESH)
        if cond is None:
            c.start()
        else:
            pl.when(cond)(c.start)
        started.append((cond, c))

    def drain(n):
        for cond, c in started[:n]:
            if cond is None:
                c.wait_send()
            else:
                pl.when(cond)(c.wait_send)
        del started[:n]

    def arrive(dst, ss, rs):
        pltpu.make_async_remote_copy(src_ref=dst, dst_ref=dst, send_sem=ss, recv_sem=rs, device_id=sib, device_id_type=MESH).wait_recv()

    loads = [
        pltpu.make_async_copy(a, b, loc.at[i])
        for i, (a, b) in enumerate([(og, og_v), (pre, pre_v), (w_out_hbm, w_out), (w_in_hbm, w_in), (li, li_v)])
    ]
    for c in loads:
        c.start()

    barrier = pltpu.get_barrier_semaphore()
    greet = [dev(x=(x + a) % 4, zh=(zh + b) % 4) for a in range(4) for b in range(4) if (a, b) != (0, 0)]
    greet += [dev(x=(x + a) % 4, k=1 - k) for a in (1, 2, 3)] + ynext + [sib, zpart]
    for p in greet:
        pl.semaphore_signal(barrier, inc=1, device_id=p, device_id_type=MESH)
    loads[0].wait()
    pl.semaphore_wait(barrier, len(greet))

    def in_z(own, full, ss, rs):
        full[k, my] = own[...]
        for dz in (2, 1, 3):
            send(own, full.at[k, my], ss.at[dz - 1], rs.at[dz - 1], dev(zh=(zh + dz) % 4))

    def in_x(full, zss, zrs, ss, rs):
        for dz in (0, 1, 3, 2):
            ref = full.at[k, 4 * x + (zh + 4 - dz) % 4]
            if dz > 0:
                arrive(ref, zss.at[dz - 1], zrs.at[dz - 1])
            for dx in (2, 1, 3, 0):
                send(ref, ref, ss.at[dx, dz], rs.at[dx, dz], dev(x=(x + dx) % 4, k=1 - k))

    def in_core(full, xss, xrs, ss, rs):
        for dx in (0, 1, 3, 2):
            xs = (x + 4 - dx) % 4
            for dz in range(4):
                arrive(full.at[1 - k, 4 * xs + (zh + 4 - dz) % 4], xss.at[dx, dz], xrs.at[dx, dz])
            if dx > 0:
                ref = full.at[1 - k, pl.ds(4 * xs, 4)]
                send(ref, ref, ss.at[dx - 1], rs.at[dx - 1], sib)

    def in_done(full, ss, rs):
        for dx in (1, 3, 2):
            arrive(full.at[k, pl.ds(4 * ((x + 4 - dx) % 4), 4)], ss.at[dx - 1], rs.at[dx - 1])

    def swap(full, a, ss, rs):
        ref = full.at[halves[a], col]
        send(ref, ref, ss.at[a], rs.at[a], zpart)

    def ring(full, j, s, a, zss, zrs, ss, rs):
        zz = zl if j == 0 else 1 - zl
        if j == 1 and s == 0:
            arrive(full.at[halves[a], 2 * y + zz], zss.at[a], zrs.at[a])
        for d in range(2):
            hops = 4 if a == d else 3
            ref = full.at[halves[a], 2 * ((y + (8 - s if d == 0 else s)) % 8) + zz]
            if 0 < s <= hops:
                arrive(ref, ss.at[j, d, s - 1, a], rs.at[j, d, s - 1, a])
            if s < hops:
                send(ref, ref, ss.at[j, d, s, a], rs.at[j, d, s, a], ynext[d])

    in_z(og_v, og_all, oz_ss, oz_rs)
    loads[1].wait()
    for h in range(2):
        value, sl = gelu_parts(pre_v[pl.ds(h * T, T), :].astype(F32))
        act_all[h, col] = value.astype(BF)
        slope[h] = sl

    def act_step(j, s):
        for a in range(2):
            if j == 0 and s == 0:
                swap(act_all, a, az_ss, az_rs)
            ring(act_all, j, s, a, az_ss, az_rs, ay_ss, ay_rs)

    def hid_step(j, s, a):
        ring(hid_all, j, s, a, hz_ss, hz_rs, hy_ss, hy_rs)

    act_step(0, 0)
    act_step(0, 1)
    act_step(1, 0)
    in_x(og_all, oz_ss, oz_rs, ox_ss, ox_rs)
    act_step(1, 1)
    act_step(0, 2)
    loads[4].wait()
    in_core(og_all, ox_ss, ox_rs, os_ss, os_rs)

    def partial(a, n):
        return dot(og_all[halves[a]].reshape(16 * T, DB), w_out[pl.ds(n * FT, FT), :], 1, 1).reshape(8, 2, T, FT)

    def to_partner(a, s):
        h = halves[a]
        for o in (((4, 5), (3, 6), (2, 7), (1, 0)), ((4, 3), (5, 2), (6, 1), (7, 0)))[a][s]:
            at = (y + o) % 8
            cz_send[h, at] = c_a[h, at, 1 - zl].astype(BF)
            send(cz_send.at[h, at], cz_recv.at[h, at], cz_ss.at[o, a], cz_rs.at[o, a], zpart)

    def partials(a):
        h = halves[a]
        for n in (1, 2):
            c_a[h, :, :, :, pl.ds(n * FT - FT, FT)] = partial(a, n)
        to_partner(a, 0)
        to_partner(a, 1)
        c_b[h] = partial(a, 0)
        rs_b(a, 0)

    def rs_b(a, s):
        h = halves[a]
        for d in range(2):
            hops = 3 if a == d else 4
            if s >= hops:
                continue
            to = hops - s
            total = c_b[h, (y + (to if d == 0 else 8 - to)) % 8]
            if s > 0:
                arrive(rb_recv.at[d, s - 1, a], rb_ss.at[d, s - 1, a], rb_rs.at[d, s - 1, a])
                total = total + rb_recv[d, s - 1, a].astype(F32)
            rb_send[d, s, a] = total.astype(BF)
            send(rb_send.at[d, s, a], rb_recv.at[d, s, a], rb_ss.at[d, s, a], rb_rs.at[d, s, a], ynext[d])

    def mine(a, o):
        h, at = halves[a], (y + o) % 8
        arrive(cz_recv.at[h, at], cz_ss.at[o, a], cz_rs.at[o, a])
        return c_a[h, at, zl] + cz_recv[h, at].astype(F32)

    def rs_a(a, s):
        for d in range(2):
            hops = 4 if a == d else 3
            if s >= hops:
                continue
            to = hops - s
            total = mine(a, to if d == 0 else 8 - to)
            if s > 0:
                arrive(ra_recv.at[d, s - 1, a], ra_ss.at[d, s - 1, a], ra_rs.at[d, s - 1, a])
                total = total + ra_recv[d, s - 1, a].astype(F32)
            ra_send[d, s, a] = total.astype(BF)
            send(ra_send.at[d, s, a], ra_recv.at[d, s, a], ra_ss.at[d, s, a], ra_rs.at[d, s, a], ynext[d])
        if s < 2:
            to_partner(a, s + 2)

    def last_b(a):
        h = halves[a]
        for d in range(2):
            s = 2 if a == d else 3
            arrive(rb_recv.at[d, s, a], rb_ss.at[d, s, a], rb_rs.at[d, s, a])
        bz_send[a] = (c_b[h, y, 1 - zl] + rb_recv[0, 2 if a == 0 else 3, a, 1 - zl].astype(F32) + rb_recv[1, 2 if a == 1 else 3, a, 1 - zl].astype(F32)).astype(BF)
        send(bz_send.at[a], bz_recv.at[a], bz_ss.at[a], bz_rs.at[a], zpart)

    def last_a(a):
        h = halves[a]
        total = mine(a, 0)
        for d in range(2):
            s = 3 if a == d else 2
            arrive(ra_recv.at[d, s, a], ra_ss.at[d, s, a], ra_rs.at[d, s, a])
            total = total + ra_recv[d, s, a].astype(F32)
        hid_all[h, col, :, pl.ds(FT, FA)] = (total * slope[h, :, pl.ds(FT, FA)]).astype(BF)
        total = c_b[h, y, zl] + rb_recv[0, 2 if a == 0 else 3, a, zl].astype(F32) + rb_recv[1, 2 if a == 1 else 3, a, zl].astype(F32)
        arrive(bz_recv.at[a], bz_ss.at[a], bz_rs.at[a])
        total = total + bz_recv[a].astype(F32)
        hid_all[h, col, :, pl.ds(0, FT)] = (total * slope[h, :, pl.ds(0, FT)]).astype(BF)

    loads[2].wait()
    partials(0)
    act_step(1, 2)
    act_step(0, 3)
    in_done(og_all, os_ss, os_rs)
    partials(1)
    in_z(li_v, li_all, lz_ss, lz_rs)
    rs_a(0, 0)
    rs_a(1, 0)
    rs_b(0, 1)
    rs_b(1, 1)
    rs_a(0, 1)
    rs_a(1, 1)
    act_step(1, 3)
    rs_b(0, 2)
    rs_b(1, 2)
    rs_a(0, 2)
    rs_a(1, 2)
    rs_b(0, 3)
    rs_b(1, 3)
    rs_a(0, 3)
    rs_a(1, 3)
    in_x(li_all, lz_ss, lz_rs, lx_ss, lx_rs)
    last_b(0)
    last_b(1)

    def q_part(a, offs):
        h = halves[a]
        at = [2 * ((y + o) % 8) for o in offs]
        rows = jnp.concatenate([hid_all[h, pl.ds(p, 2)].reshape(2 * T, FB) for p in at], axis=0)
        q = dot(rows, w_in[...], 1, 1)
        for i, (o, p) in enumerate(zip(offs, at, strict=True)):
            part = q[2 * i * T : 2 * (i + 1) * T].reshape(2, T, DB)
            if a == 0:
                q_sib[pl.ds(p, 2)] = part
                send(q_sib.at[pl.ds(p, 2)], q_in.at[pl.ds(p, 2)], qs_ss.at[o], qs_rs.at[o], sib)
                continue
            arrive(q_in.at[pl.ds(p, 2)], qs_ss.at[o], qs_rs.at[o])
            part = part + q_in[pl.ds(p, 2)]
            q_send[pl.ds(p, 2)] = part.astype(BF)
            for b in range(2):
                stays = p + b == my

                @pl.when(stays)
                def _():
                    q_self[...] = part[b]

                px, pz = (p + b) // 4, (p + b) % 4
                slot = (px + 4 - x) % 4 * 4 + (pz + 4 - zh) % 4
                send(q_send.at[p + b], q_recv.at[slot], q_ss.at[o, b], q_rs.at[slot], dev(x=px, zh=pz), jnp.logical_not(stays))

    def go_tile(n):
        cols = pl.ds(n * FT, FT)
        go_out[cols, :] = dot(act_all[:, :, :, cols].reshape(TOK, FT), og_all[...].reshape(TOK, DB), 0, 0)

    old = len(started)
    for a in range(2):
        last_a(a)
        swap(hid_all, a, hz_ss, hz_rs)
        hid_step(0, 0, a)
    act_step(0, 4)
    act_step(1, 4)
    go_tile(0)
    hid_step(1, 0, 0)
    hid_step(1, 0, 1)
    for j in range(2):
        hid_step(j, 1, 0)
        hid_step(j, 1, 1)
    go_tile(1)
    drain(old)
    in_core(li_all, lx_ss, lx_rs, ls_ss, ls_rs)
    loads[3].wait()
    for j in range(2):
        hid_step(j, 2, 0)
        hid_step(j, 2, 1)
    q_part(0, (0, 1, 7, 2, 6))
    for j in range(2):
        hid_step(j, 3, 0)
        hid_step(j, 3, 1)
    q_part(1, (0, 1, 7, 2, 6))
    q_part(0, (3, 5))
    hid_step(0, 4, 0)
    hid_step(0, 4, 1)
    q_part(1, (3, 5))
    hid_step(1, 4, 0)
    old = len(started)
    q_part(0, (4,))
    hid_step(1, 4, 1)
    q_part(1, (4,))
    go_tile(2)
    in_done(li_all, ls_ss, ls_rs)
    li_t[...] = li_all[...].reshape(TOK, DB).T
    for n in range(3):
        cols = pl.ds(n * FT, FT)
        gi_out[:, cols] = dot(li_t[...], hid_all[:, :, :, cols].reshape(TOK, FT), 1, 0)
    drain(old)
    total = q_self[...]
    for j in range(1, 16):
        arrive(q_recv.at[j], q_ss.at[0, 0], q_rs.at[j])
        total = total + q_recv[j].astype(F32)
    ig_out[...] = total.astype(BF)
    drain(len(started))


def on_device(layer_input, output_grad, preact, weight_in, weight_out):
    vmem, dma = pltpu.VMEM, pltpu.SemaphoreType.DMA
    ins = [pltpu.with_memory_space_constraint(a, pltpu.HBM) for a in (layer_input, output_grad, preact, weight_in, weight_out)]
    gather = [(3,), (3,), (4, 4), (4, 4), (3,), (3,)]
    sems = gather + gather
    sems += [s for s in [(2,), (2, 2, 4, 2), (2, 2, 4, 2), (2,), (8, 2), (2, 4, 2), (2, 4, 2), (2,), (8,)] for _ in range(2)]
    sems += [(8, 2), (16,), (5,)]
    return pl.pallas_call(
        kernel,
        out_shape=(
            jax.ShapeDtypeStruct((T, DB), BF),
            jax.ShapeDtypeStruct((DB, FB), F32),
            jax.ShapeDtypeStruct((FB, DB), F32),
        ),
        in_specs=[pl.BlockSpec(memory_space=pltpu.HBM)] * 5,
        out_specs=(pl.BlockSpec(memory_space=pltpu.VMEM),) * 3,
        scratch_shapes=[
            vmem((T, DB), BF),
            vmem((T, DB), BF),
            vmem((2 * T, FB), BF),
            vmem((DB, FB), BF),
            vmem((FB, DB), BF),
            vmem((2, 16, T, DB), BF),
            vmem((2, 16, T, DB), BF),
            vmem((2, 16, T, FB), BF),
            vmem((2, 16, T, FB), BF),
            vmem((DB, TOK), BF),
            vmem((2, T, FB), F32),
            vmem((2, 8, 2, T, FA), F32),
            vmem((2, 8, 2, T, FT), F32),
            vmem((2, 8, T, FA), BF),
            vmem((2, 8, T, FA), BF),
            vmem((2, 4, 2, T, FA), BF),
            vmem((2, 4, 2, T, FA), BF),
            vmem((2, 4, 2, 2, T, FT), BF),
            vmem((2, 4, 2, 2, T, FT), BF),
            vmem((2, T, FT), BF),
            vmem((2, T, FT), BF),
            vmem((16, T, DB), F32),
            vmem((16, T, DB), F32),
            vmem((16, T, DB), BF),
            vmem((16, T, DB), BF),
            vmem((T, DB), F32),
        ]
        + [dma(s) for s in sems],
        compiler_params=pltpu.CompilerParams(collective_id=0, has_side_effects=True, vmem_limit_bytes=48 * 2**20),
        cost_estimate=pl.CostEstimate(flops=8 * TOK * DB * FB, bytes_accessed=4 * 2**20, transcendentals=2 * 64 * FB),
        name="mlp_backward",
    )(*ins)


def solution(mesh):
    in_specs = (P("row", "col"), P("row", "col"), P("col", "row"), P("col", "row"), P("row", "col"))
    out_specs = (P("row", "col"), P("col", "row"), P("row", "col"))
    return jax.shard_map(on_device, mesh=mesh, in_specs=in_specs, out_specs=out_specs, check_vma=False)
```

```python
import math

import jax
import jax.numpy as jnp
from jax import lax
from jax.experimental import pallas as pl
from jax.experimental.pallas import tpu as pltpu
from jax.sharding import PartitionSpec as P

MESH = pl.DeviceIdType.MESH
BF, F32 = jnp.bfloat16, jnp.float32
TOK, DB, FB = 1024, 384, 768
T = 32
FT = 256
FA = 512


def gelu_parts(pre):
    cdf = 0.5 * (1.0 + lax.erf(pre * (1.0 / math.sqrt(2.0))))
    pdf = jnp.exp(-0.5 * pre * pre) * (1.0 / math.sqrt(2.0 * math.pi))
    return pre * cdf, cdf + pre * pdf


def dot(a, b, ca, cb):
    return lax.dot_general(a, b, (((ca,), (cb,)), ((), ())), preferred_element_type=F32)


def kernel(
    li, og, pre, w_in_hbm, w_out_hbm, ig_out, gi_out, go_out,
    li_v, og_v, pre_v, w_in, w_out, li_all, og_all, act_all, hid_all, li_t, slope, c_a, c_b, cz_send, cz_recv,
    ra_send, ra_recv, rb_send, rb_recv, bz_send, bz_recv, q_sib, q_in, q_send, q_recv, q_self,
    oz_ss, oz_rs, ox_ss, ox_rs, os_ss, os_rs, lz_ss, lz_rs, lx_ss, lx_rs, ls_ss, ls_rs,
    az_ss, az_rs, ay_ss, ay_rs, hy_ss, hy_rs, hz_ss, hz_rs, hp_ss, hp_rs, cz_ss, cz_rs, ra_ss, ra_rs, rb_ss, rb_rs, bz_ss, bz_rs,
    qs_ss, qs_rs, q_ss, q_rs, loc,
):
    row, col = lax.axis_index("row"), lax.axis_index("col")
    x, zh, k = row // 8, (row // 2) % 4, row % 2
    y, zl = col // 2, col % 2
    halves = (1 - k, k)
    my = 4 * x + zh

    def dev(x=x, zh=zh, k=k, y=y, zl=zl):
        return (x * 8 + zh * 2 + k, y * 2 + zl)

    sib, zpart = dev(k=1 - k), dev(zl=1 - zl)
    ynext = [dev(y=(y + 1) % 8), dev(y=(y + 7) % 8)]
    started = []

    def send(src, dst, ss, rs, to, cond=None):
        c = pltpu.make_async_remote_copy(src_ref=src, dst_ref=dst, send_sem=ss, recv_sem=rs, device_id=to, device_id_type=MESH)
        if cond is None:
            c.start()
        else:
            pl.when(cond)(c.start)
        started.append((cond, c))

    def drain(n):
        for cond, c in started[:n]:
            if cond is None:
                c.wait_send()
            else:
                pl.when(cond)(c.wait_send)
        del started[:n]

    def arrive(dst, ss, rs):
        pltpu.make_async_remote_copy(src_ref=dst, dst_ref=dst, send_sem=ss, recv_sem=rs, device_id=sib, device_id_type=MESH).wait_recv()

    loads = [
        pltpu.make_async_copy(a, b, loc.at[i])
        for i, (a, b) in enumerate([(og, og_v), (pre, pre_v), (w_out_hbm, w_out), (w_in_hbm, w_in), (li, li_v)])
    ]
    for c in loads:
        c.start()

    barrier = pltpu.get_barrier_semaphore()
    greet = [dev(x=(x + a) % 4, zh=(zh + b) % 4) for a in range(4) for b in range(4) if (a, b) != (0, 0)]
    greet += [dev(x=(x + a) % 4, k=1 - k) for a in (1, 2, 3)] + ynext + [sib, zpart]
    for p in greet:
        pl.semaphore_signal(barrier, inc=1, device_id=p, device_id_type=MESH)
    loads[0].wait()
    pl.semaphore_wait(barrier, len(greet))

    def in_z(own, full, ss, rs):
        full[k, my] = own[...]
        for dz in (2, 1, 3):
            send(own, full.at[k, my], ss.at[dz - 1], rs.at[dz - 1], dev(zh=(zh + dz) % 4))

    def in_x(full, zss, zrs, ss, rs):
        for dz in (0, 1, 3, 2):
            ref = full.at[k, 4 * x + (zh + 4 - dz) % 4]
            if dz > 0:
                arrive(ref, zss.at[dz - 1], zrs.at[dz - 1])
            for dx in (2, 1, 3, 0):
                send(ref, ref, ss.at[dx, dz], rs.at[dx, dz], dev(x=(x + dx) % 4, k=1 - k))

    def in_core(full, xss, xrs, ss, rs):
        for dx in (0, 1, 3, 2):
            xs = (x + 4 - dx) % 4
            for dz in range(4):
                arrive(full.at[1 - k, 4 * xs + (zh + 4 - dz) % 4], xss.at[dx, dz], xrs.at[dx, dz])
            if dx > 0:
                ref = full.at[1 - k, pl.ds(4 * xs, 4)]
                send(ref, ref, ss.at[dx - 1], rs.at[dx - 1], sib)

    def in_done(full, ss, rs):
        for dx in (1, 3, 2):
            arrive(full.at[k, pl.ds(4 * ((x + 4 - dx) % 4), 4)], ss.at[dx - 1], rs.at[dx - 1])

    def swap(full, a, ss, rs):
        ref = full.at[halves[a], col]
        send(ref, ref, ss.at[a], rs.at[a], zpart)

    def ring(full, j, s, a, zss, zrs, ss, rs, reach=4):
        zz = zl if j == 0 else 1 - zl
        if j == 1 and s == 0:
            arrive(full.at[halves[a], 2 * y + zz], zss.at[a], zrs.at[a])
        for d in range(2):
            hops = min(4 if a == d else 3, reach)
            ref = full.at[halves[a], 2 * ((y + (8 - s if d == 0 else s)) % 8) + zz]
            if 0 < s <= hops:
                arrive(ref, ss.at[j, d, s - 1, a], rs.at[j, d, s - 1, a])
            if s < hops:
                send(ref, ref, ss.at[j, d, s, a], rs.at[j, d, s, a], ynext[d])

    in_z(og_v, og_all, oz_ss, oz_rs)
    loads[1].wait()
    for h in range(2):
        value, sl = gelu_parts(pre_v[pl.ds(h * T, T), :].astype(F32))
        act_all[h, col] = value.astype(BF)
        slope[h] = sl

    def act_step(j, s):
        for a in range(2):
            if j == 0 and s == 0:
                swap(act_all, a, az_ss, az_rs)
            ring(act_all, j, s, a, az_ss, az_rs, ay_ss, ay_rs)

    def hid_step(j, s, a):
        ring(hid_all, j, s, a, hz_ss, hz_rs, hy_ss, hy_rs, 4 if j == 0 else 2)
        if j == 0 and s >= 3:
            for o in (5, 3) if s == 3 else (4,):
                ref = hid_all.at[halves[a], 2 * ((y + o) % 8) + zl]
                send(ref, ref, hp_ss.at[o - 3, a], hp_rs.at[o - 3, a], zpart)

    def passed(a, offs):
        for o in offs:
            ref = hid_all.at[halves[a], 2 * ((y + o) % 8) + 1 - zl]
            arrive(ref, hp_ss.at[o - 3, a], hp_rs.at[o - 3, a])

    act_step(0, 0)
    act_step(0, 1)
    act_step(1, 0)
    in_x(og_all, oz_ss, oz_rs, ox_ss, ox_rs)
    act_step(1, 1)
    act_step(0, 2)
    loads[4].wait()
    in_core(og_all, ox_ss, ox_rs, os_ss, os_rs)

    def partial(a, n):
        return dot(og_all[halves[a]].reshape(16 * T, DB), w_out[pl.ds(n * FT, FT), :], 1, 1).reshape(8, 2, T, FT)

    def to_partner(a, s):
        h = halves[a]
        for o in (((4, 5), (3, 6), (2, 7), (1, 0)), ((4, 3), (5, 2), (6, 1), (7, 0)))[a][s]:
            at = (y + o) % 8
            cz_send[h, at] = c_a[h, at, 1 - zl].astype(BF)
            send(cz_send.at[h, at], cz_recv.at[h, at], cz_ss.at[o, a], cz_rs.at[o, a], zpart)

    def partials(a):
        h = halves[a]
        for n in (1, 2):
            c_a[h, :, :, :, pl.ds(n * FT - FT, FT)] = partial(a, n)
        to_partner(a, 0)
        to_partner(a, 1)
        c_b[h] = partial(a, 0)
        rs_b(a, 0)

    def rs_b(a, s):
        h = halves[a]
        for d in range(2):
            hops = 3 if a == d else 4
            if s >= hops:
                continue
            to = hops - s
            total = c_b[h, (y + (to if d == 0 else 8 - to)) % 8]
            if s > 0:
                arrive(rb_recv.at[d, s - 1, a], rb_ss.at[d, s - 1, a], rb_rs.at[d, s - 1, a])
                total = total + rb_recv[d, s - 1, a].astype(F32)
            rb_send[d, s, a] = total.astype(BF)
            send(rb_send.at[d, s, a], rb_recv.at[d, s, a], rb_ss.at[d, s, a], rb_rs.at[d, s, a], ynext[d])

    def mine(a, o):
        h, at = halves[a], (y + o) % 8
        arrive(cz_recv.at[h, at], cz_ss.at[o, a], cz_rs.at[o, a])
        return c_a[h, at, zl] + cz_recv[h, at].astype(F32)

    def rs_a(a, s):
        for d in range(2):
            hops = 4 if a == d else 3
            if s >= hops:
                continue
            to = hops - s
            total = mine(a, to if d == 0 else 8 - to)
            if s > 0:
                arrive(ra_recv.at[d, s - 1, a], ra_ss.at[d, s - 1, a], ra_rs.at[d, s - 1, a])
                total = total + ra_recv[d, s - 1, a].astype(F32)
            ra_send[d, s, a] = total.astype(BF)
            send(ra_send.at[d, s, a], ra_recv.at[d, s, a], ra_ss.at[d, s, a], ra_rs.at[d, s, a], ynext[d])
        if s < 2:
            to_partner(a, s + 2)

    def last_b(a):
        h = halves[a]
        for d in range(2):
            s = 2 if a == d else 3
            arrive(rb_recv.at[d, s, a], rb_ss.at[d, s, a], rb_rs.at[d, s, a])
        bz_send[a] = (c_b[h, y, 1 - zl] + rb_recv[0, 2 if a == 0 else 3, a, 1 - zl].astype(F32) + rb_recv[1, 2 if a == 1 else 3, a, 1 - zl].astype(F32)).astype(BF)
        send(bz_send.at[a], bz_recv.at[a], bz_ss.at[a], bz_rs.at[a], zpart)

    def last_a(a):
        h = halves[a]
        total = mine(a, 0)
        for d in range(2):
            s = 3 if a == d else 2
            arrive(ra_recv.at[d, s, a], ra_ss.at[d, s, a], ra_rs.at[d, s, a])
            total = total + ra_recv[d, s, a].astype(F32)
        hid_all[h, col, :, pl.ds(FT, FA)] = (total * slope[h, :, pl.ds(FT, FA)]).astype(BF)
        total = c_b[h, y, zl] + rb_recv[0, 2 if a == 0 else 3, a, zl].astype(F32) + rb_recv[1, 2 if a == 1 else 3, a, zl].astype(F32)
        arrive(bz_recv.at[a], bz_ss.at[a], bz_rs.at[a])
        total = total + bz_recv[a].astype(F32)
        hid_all[h, col, :, pl.ds(0, FT)] = (total * slope[h, :, pl.ds(0, FT)]).astype(BF)

    loads[2].wait()
    partials(0)
    act_step(1, 2)
    act_step(0, 3)
    in_done(og_all, os_ss, os_rs)
    partials(1)
    in_z(li_v, li_all, lz_ss, lz_rs)
    rs_a(0, 0)
    rs_a(1, 0)
    rs_b(0, 1)
    rs_b(1, 1)
    rs_a(0, 1)
    rs_a(1, 1)
    act_step(1, 3)
    rs_b(0, 2)
    rs_b(1, 2)
    rs_a(0, 2)
    rs_a(1, 2)
    rs_b(0, 3)
    rs_b(1, 3)
    rs_a(0, 3)
    rs_a(1, 3)
    in_x(li_all, lz_ss, lz_rs, lx_ss, lx_rs)
    last_b(0)
    last_b(1)

    def q_part(a, offs):
        h = halves[a]
        at = [2 * ((y + o) % 8) for o in offs]
        rows = jnp.concatenate([hid_all[h, pl.ds(p, 2)].reshape(2 * T, FB) for p in at], axis=0)
        q = dot(rows, w_in[...], 1, 1)
        for i, (o, p) in enumerate(zip(offs, at, strict=True)):
            part = q[2 * i * T : 2 * (i + 1) * T].reshape(2, T, DB)
            if a == 0:
                q_sib[pl.ds(p, 2)] = part
                send(q_sib.at[pl.ds(p, 2)], q_in.at[pl.ds(p, 2)], qs_ss.at[o], qs_rs.at[o], sib)
                continue
            arrive(q_in.at[pl.ds(p, 2)], qs_ss.at[o], qs_rs.at[o])
            part = part + q_in[pl.ds(p, 2)]
            q_send[pl.ds(p, 2)] = part.astype(BF)
            for b in range(2):
                stays = p + b == my

                @pl.when(stays)
                def _():
                    q_self[...] = part[b]

                px, pz = (p + b) // 4, (p + b) % 4
                slot = (px + 4 - x) % 4 * 4 + (pz + 4 - zh) % 4
                send(q_send.at[p + b], q_recv.at[slot], q_ss.at[o, b], q_rs.at[slot], dev(x=px, zh=pz), jnp.logical_not(stays))

    def go_tile(n):
        cols = pl.ds(n * FT, FT)
        go_out[cols, :] = dot(act_all[:, :, :, cols].reshape(TOK, FT), og_all[...].reshape(TOK, DB), 0, 0)

    old = len(started)
    for a in range(2):
        last_a(a)
        swap(hid_all, a, hz_ss, hz_rs)
        hid_step(0, 0, a)
    act_step(0, 4)
    act_step(1, 4)
    go_tile(0)
    hid_step(1, 0, 0)
    hid_step(1, 0, 1)
    for j in range(2):
        hid_step(j, 1, 0)
        hid_step(j, 1, 1)
    go_tile(1)
    drain(old)
    in_core(li_all, lx_ss, lx_rs, ls_ss, ls_rs)
    loads[3].wait()
    for j in range(2):
        hid_step(j, 2, 0)
        hid_step(j, 2, 1)
    q_part(0, (0, 1, 7, 2, 6))
    hid_step(0, 3, 0)
    hid_step(0, 3, 1)
    q_part(1, (0, 1, 7, 2, 6))
    hid_step(0, 4, 0)
    hid_step(0, 4, 1)
    passed(0, (3, 5))
    q_part(0, (3, 5))
    passed(1, (3, 5))
    q_part(1, (3, 5))
    old = len(started)
    passed(0, (4,))
    q_part(0, (4,))
    passed(1, (4,))
    q_part(1, (4,))
    go_tile(2)
    in_done(li_all, ls_ss, ls_rs)
    li_t[...] = li_all[...].reshape(TOK, DB).T
    for n in range(3):
        cols = pl.ds(n * FT, FT)
        gi_out[:, cols] = dot(li_t[...], hid_all[:, :, :, cols].reshape(TOK, FT), 1, 0)
    drain(old)
    total = q_self[...]
    for j in range(1, 16):
        arrive(q_recv.at[j], q_ss.at[0, 0], q_rs.at[j])
        total = total + q_recv[j].astype(F32)
    ig_out[...] = total.astype(BF)
    drain(len(started))


def on_device(layer_input, output_grad, preact, weight_in, weight_out):
    vmem, dma = pltpu.VMEM, pltpu.SemaphoreType.DMA
    ins = [pltpu.with_memory_space_constraint(a, pltpu.HBM) for a in (layer_input, output_grad, preact, weight_in, weight_out)]
    gather = [(3,), (3,), (4, 4), (4, 4), (3,), (3,)]
    sems = gather + gather
    sems += [s for s in [(2,), (2, 2, 4, 2), (2, 2, 4, 2), (2,), (3, 2), (8, 2), (2, 4, 2), (2, 4, 2), (2,), (8,)] for _ in range(2)]
    sems += [(8, 2), (16,), (5,)]
    return pl.pallas_call(
        kernel,
        out_shape=(
            jax.ShapeDtypeStruct((T, DB), BF),
            jax.ShapeDtypeStruct((DB, FB), F32),
            jax.ShapeDtypeStruct((FB, DB), F32),
        ),
        in_specs=[pl.BlockSpec(memory_space=pltpu.HBM)] * 5,
        out_specs=(pl.BlockSpec(memory_space=pltpu.VMEM),) * 3,
        scratch_shapes=[
            vmem((T, DB), BF),
            vmem((T, DB), BF),
            vmem((2 * T, FB), BF),
            vmem((DB, FB), BF),
            vmem((FB, DB), BF),
            vmem((2, 16, T, DB), BF),
            vmem((2, 16, T, DB), BF),
            vmem((2, 16, T, FB), BF),
            vmem((2, 16, T, FB), BF),
            vmem((DB, TOK), BF),
            vmem((2, T, FB), F32),
            vmem((2, 8, 2, T, FA), F32),
            vmem((2, 8, 2, T, FT), F32),
            vmem((2, 8, T, FA), BF),
            vmem((2, 8, T, FA), BF),
            vmem((2, 4, 2, T, FA), BF),
            vmem((2, 4, 2, T, FA), BF),
            vmem((2, 4, 2, 2, T, FT), BF),
            vmem((2, 4, 2, 2, T, FT), BF),
            vmem((2, T, FT), BF),
            vmem((2, T, FT), BF),
            vmem((16, T, DB), F32),
            vmem((16, T, DB), F32),
            vmem((16, T, DB), BF),
            vmem((16, T, DB), BF),
            vmem((T, DB), F32),
        ]
        + [dma(s) for s in sems],
        compiler_params=pltpu.CompilerParams(collective_id=0, has_side_effects=True, vmem_limit_bytes=48 * 2**20),
        cost_estimate=pl.CostEstimate(flops=8 * TOK * DB * FB, bytes_accessed=4 * 2**20, transcendentals=2 * 64 * FB),
        name="mlp_backward",
    )(*ins)


def solution(mesh):
    in_specs = (P("row", "col"), P("row", "col"), P("col", "row"), P("col", "row"), P("row", "col"))
    out_specs = (P("row", "col"), P("col", "row"), P("row", "col"))
    return jax.shard_map(on_device, mesh=mesh, in_specs=in_specs, out_specs=out_specs, check_vma=False)
```
